32 devices in a mesh: tm: 4 (over y, x), clus: 8 (over z, core).
Axes of the slice: x: 2, y: 2, z: 4, core: 2. Of those that a mesh axis runs over, the one named last changes fastest.
Arguments:
- currents: bfloat16 [256, 256, 128], P('clus', 'tm'), may hold values from -6 to 6
- excitation: bfloat16 [256, 256, 128], P('clus', 'tm'), may hold values from -6 to 6
- neighbours: int32 [256, 30], P('clus'), may hold values from -1 to 255, as said below
- lag_profile: bfloat16 [30, 64], replicated, may hold values from -0.125 to 0.125
- couplings: bfloat16 [30, 128, 128], replicated, may hold values from -0.5 to 0.5
- block_inverses: bfloat16 [256, 128, 128], P('clus'), may hold values from -0.5 to 0.5
- charge_map: bfloat16 [128, 128], replicated, may hold values from -0.03125 to 0.03125
- potential: bfloat16 [128, 128], replicated, may hold values from -0.5 to 0.5
Outputs:
- updated: bfloat16 [256, 256, 128], P('clus', 'tm')
- residual: float32 [256, 256, 128], P('clus', 'tm')
The draws below stay inside these ranges and needn't reach their ends.
Inputs may be any that keep to these rules, and one draw needn't show every extreme that they name: `neighbours`: row j lists distinct panel clusters from j // 32 * 32 - 32 to j // 32 * 32 + 2 * 32 - 1, modulo 256; entries -1 pad the end of a row, and every row has a cluster in its first slot.
All inputs are finite; a program needn't handle non-finite values.
Results may differ from the reference program's by a relative error of at most 0.0051.
Values may be sent and summed in bfloat16 or wider, within the bound.
A program may use at most 64 MiB of HBM per device.

```python
import jax
import jax.numpy as jnp
from jax import lax

B = 128
M = 128
NB = 30
LAG = 64
CPD = 32
TB = 64
CLUSTERS = 256
STEPS = 256
N_TM = 4


def draw_neighbours(key, part):
    candidates = 3 * CPD
    first_key, second_key = jax.random.split(jax.random.fold_in(key, 11))
    scores = jax.random.randint(first_key, (CLUSTERS, candidates), 0, 1 << 20) * candidates + jnp.arange(candidates)[None, :]
    order = jnp.argsort(scores, axis=1)
    taken = min(NB, candidates)
    chosen = order[:, :taken]
    device_first = (jnp.arange(CLUSTERS) // CPD - 1) * CPD
    cluster_ids = (device_first[:, None] + chosen) % CLUSTERS
    counts = jax.random.randint(second_key, (CLUSTERS,), taken - taken // 4, taken + 1)
    cluster_ids = jnp.where(jnp.arange(taken)[None, :] < counts[:, None], cluster_ids, -1)
    if taken < NB:
        cluster_ids = jnp.concatenate([cluster_ids, -jnp.ones((CLUSTERS, NB - taken), cluster_ids.dtype)], axis=1)
    return cluster_ids.astype(jnp.int32)


def steps_of(stream_key, extent, cuts, smallest, high):
    def one(position, shards_of):
        steps = jax.random.uniform(jax.random.fold_in(jax.random.fold_in(stream_key, 6), position), (shards_of,), jnp.float32, smallest / len(cuts), high / len(cuts))
        return jnp.repeat(jnp.exp(steps), extent[position] // shards_of).reshape((-1,) + (1,) * (len(extent) - position - 1))

    level = one(*cuts[0])
    for cut in cuts[1:]:
        level = level * one(*cut)
    return level


def centred(key, dims, scale, bound, cuts=(), held_as=jnp.bfloat16):
    factor_of = steps_of(key, dims, cuts, -0.22, 0.18) if cuts else 1.0
    array = jax.random.normal(key, dims, jnp.float32) * scale * factor_of
    return jnp.minimum(jnp.maximum(array, -bound), bound).astype(held_as)


def setup_inputs(seed: int = 0) -> dict:
    key_of = jax.random.split(jax.random.key(seed), 9)
    currents = centred(key_of[0], (CLUSTERS, STEPS, B), 1.0, 6.0, ((0, 8), (1, 4)))
    excitation = centred(key_of[1], (CLUSTERS, STEPS, B), 1.0, 6.0, ((0, 8), (1, 4)))
    neighbours = draw_neighbours(jax.random.fold_in(key_of[8], 71), 0)
    lag_profile = centred(key_of[3], (NB, LAG), (NB * LAG) ** -0.5, 0.125)
    couplings = centred(key_of[4], (NB, B, B), B ** -0.5, 0.5)
    block_inverses = centred(key_of[5], (CLUSTERS, B, B), B ** -0.5, 0.5, ((0, 8),))
    charge_map = centred(key_of[6], (B, M), (B * STEPS) ** -0.5, 0.03125)
    potential = centred(key_of[7], (M, B), M ** -0.5, 0.5)
    return dict(currents=currents, excitation=excitation, neighbours=neighbours, lag_profile=lag_profile, couplings=couplings, block_inverses=block_inverses, charge_map=charge_map, potential=potential)


def reference(currents, excitation, neighbours, lag_profile, couplings, block_inverses, charge_map, potential):
    clusters, steps, unknowns = currents.shape
    slot_count = lag_profile.shape[0]
    window = TB + LAG
    current32 = currents.astype(jnp.float32)
    padded = jnp.concatenate([jnp.zeros((clusters, LAG, unknowns), jnp.float32), current32], axis=1)
    present = neighbours >= 0
    safe_ids = jnp.where(present, neighbours, 0).astype(jnp.int32)
    present_f = present.astype(jnp.float32)
    lag_index = jnp.arange(TB)[:, None] + LAG - jnp.arange(window)[None, :]
    lag_onehot = (lag_index[:, :, None] == jnp.arange(LAG)[None, None, :]).astype(jnp.float32)
    toeplitz = jnp.einsum('kl,tsl->kts', lag_profile.astype(jnp.float32), lag_onehot)
    coupling = couplings.astype(jnp.float32)

    def block_field(block_index):
        start = (block_index * TB).astype(jnp.int32)
        window_slab = lax.dynamic_slice_in_dim(padded, start, window, axis=1)

        def slot_step(accum, slot):
            gathered = jnp.take(window_slab, safe_ids[:, slot], axis=0)
            filtered = jnp.einsum('ts,csb->ctb', toeplitz[slot], gathered) * present_f[:, slot][:, None, None]
            filtered = lax.optimization_barrier(filtered.astype(jnp.bfloat16)).astype(jnp.float32)
            return accum + jnp.einsum('ctb,bd->ctd', filtered, coupling[slot]), None

        start_field = jnp.zeros((clusters, TB, unknowns), jnp.float32)
        near_block, _ = lax.scan(slot_step, start_field, jnp.arange(slot_count).astype(jnp.int32))
        return near_block

    near_field = lax.map(block_field, jnp.arange(N_TM).astype(jnp.int32))
    near_field = jnp.transpose(near_field, (1, 0, 2, 3)).reshape(clusters, steps, unknowns)
    increments = jnp.dot(currents.reshape(-1, unknowns), charge_map, preferred_element_type=jnp.float32)
    increments = increments.reshape(clusters, steps, -1)
    charge = jnp.cumsum(increments, axis=1)
    charge_rounded = charge.astype(jnp.bfloat16)
    charge_field = jnp.dot(charge_rounded.reshape(clusters * steps, -1), potential, preferred_element_type=jnp.float32)
    charge_field = charge_field.reshape(clusters, steps, unknowns)
    residual = excitation.astype(jnp.float32) - near_field - charge_field
    residual_rounded = residual.astype(jnp.bfloat16)
    correction = jnp.einsum('ctb,cbd->ctd', residual_rounded.astype(jnp.float32), block_inverses.astype(jnp.float32))
    updated = (current32 + correction).astype(jnp.bfloat16)
    return updated, residual
```

```python
import jax
import jax.numpy as jnp
from jax import lax
from jax.experimental import pallas as pl
from jax.experimental.pallas import tpu as pltpu
from jax.sharding import PartitionSpec as P

GROUP = 4


def sweep_kernel(
    ids, own, prev, left, left_prev, right, right_prev, exc, toep, coup, binv, cmap, pot, before,
    upd, res, ext, filt, lower, sems,
):
    group = pl.program_id(0)
    per_dev, steps, unknowns = own.shape
    slots, _, window = toep.shape
    lags = window - steps

    @pl.when(group == 0)
    def _():
        copies = []
        for n, (old, new) in enumerate(((left_prev, left), (prev, own), (right_prev, right))):
            rows = pl.ds(n * per_dev, per_dev)
            copies.append(
                pltpu.make_async_copy(old, ext.at[rows, pl.ds(0, lags)], sems.at[2 * n])
            )
            copies.append(
                pltpu.make_async_copy(new, ext.at[rows, pl.ds(lags, steps)], sems.at[2 * n + 1])
            )
        for copy in copies:
            copy.start()
        ext[3 * per_dev] = jnp.zeros((window, unknowns), ext.dtype)
        size = GROUP * steps
        row = lax.broadcasted_iota(jnp.int32, (size, size), 0)
        col = lax.broadcasted_iota(jnp.int32, (size, size), 1)
        keep = (row >= col) & (row // steps == col // steps)
        lower[...] = jnp.where(keep, 1.0, 0.0).astype(lower.dtype)
        for copy in copies:
            copy.wait()

    first = group * GROUP
    for k in range(slots):
        for c in range(0, GROUP, 2):
            one = ext[ids[first + c, k]]
            two = ext[ids[first + c + 1, k]]
            both = jnp.concatenate([one, two], axis=1)
            out = jnp.dot(toep[k], both, preferred_element_type=jnp.float32)
            out = out.astype(jnp.bfloat16)
            lanes = pl.ds(k * unknowns, unknowns)
            filt[pl.ds(c * steps, steps), lanes] = out[:, :unknowns]
            filt[pl.ds((c + 1) * steps, steps), lanes] = out[:, unknowns:]
    near = jnp.dot(filt[...], coup[...], preferred_element_type=jnp.float32)

    own_rows = ext[pl.ds(per_dev + first, GROUP), pl.ds(lags, steps)]
    own_rows = own_rows.reshape(GROUP * steps, unknowns)
    incr = jnp.dot(own_rows, cmap[...], preferred_element_type=jnp.float32)
    high = incr.astype(jnp.bfloat16)
    rest = (incr - high.astype(jnp.float32)).astype(jnp.bfloat16)
    sums = jnp.dot(
        lower[...], jnp.concatenate([high, rest], axis=1), preferred_element_type=jnp.float32
    )
    patches = incr.shape[1]
    running = (sums[:, :patches] + sums[:, patches:]).reshape(GROUP, steps, patches)
    charge = (running + before[...][:, None, :]).astype(jnp.bfloat16)
    field = jnp.dot(
        charge.reshape(GROUP * steps, patches), pot[...], preferred_element_type=jnp.float32
    )
    residual = (
        exc[...].astype(jnp.float32).reshape(GROUP * steps, unknowns) - near - field
    )
    res[...] = residual.reshape(GROUP, steps, unknowns)
    rounded = residual.astype(jnp.bfloat16)
    for c in range(GROUP):
        rows = slice(c * steps, (c + 1) * steps)
        step = jnp.dot(rounded[rows], binv[c], preferred_element_type=jnp.float32)
        upd[c] = (own_rows[rows].astype(jnp.float32) + step).astype(upd.dtype)


def on_device(
    currents, excitation, neighbours, lag_profile, couplings, block_inverses, charge_map, potential
):
    per_dev, steps, unknowns = currents.shape
    slots, lags = lag_profile.shape
    window = steps + lags
    patches = charge_map.shape[1]
    n_tm, n_clus = lax.axis_size("tm"), lax.axis_size("clus")
    total = per_dev * n_clus

    def sent(x, by_tm, by_clus):
        pairs = [
            (t * n_clus + c, (t + by_tm) * n_clus + (c + by_clus) % n_clus)
            for t in range(n_tm - by_tm)
            for c in range(n_clus)
        ]
        return lax.ppermute(x, ("tm", "clus"), pairs)

    left = sent(currents, 0, 1)
    right = sent(currents, 0, -1)
    left_prev = sent(currents, 1, 1)
    right_prev = sent(currents, 1, -1)
    prev = sent(currents, 1, 0)

    totals = jnp.dot(
        jnp.sum(currents.astype(jnp.float32), axis=1),
        charge_map.astype(jnp.float32),
        precision=lax.Precision.HIGHEST,
    )
    before = jnp.zeros_like(totals)
    for by in range(1, n_tm):
        before = before + sent(totals, by, 0)

    first_local = (lax.axis_index("clus") - 1) * per_dev
    ids = jnp.where(neighbours >= 0, (neighbours - first_local) % total, 3 * per_dev)
    lag_index = jnp.arange(steps)[:, None] + lags - jnp.arange(window)[None, :]
    onehot = (lag_index[:, :, None] == jnp.arange(lags)[None, None, :]).astype(jnp.bfloat16)
    toep = jnp.einsum(
        "kl,tsl->kts", lag_profile, onehot, preferred_element_type=jnp.float32
    ).astype(jnp.bfloat16)

    anywhere = pl.BlockSpec(memory_space=pl.ANY)

    def whole(*shape):
        return pl.BlockSpec(shape, lambda g, ids: (0,) * len(shape))

    def grouped(*shape):
        return pl.BlockSpec((GROUP,) + shape, lambda g, ids: (g,) + (0,) * len(shape))

    size = GROUP * steps
    pairs = per_dev * slots * steps * unknowns
    return pl.pallas_call(
        sweep_kernel,
        grid_spec=pltpu.PrefetchScalarGridSpec(
            num_scalar_prefetch=1,
            grid=(per_dev // GROUP,),
            in_specs=[anywhere] * 6
            + [
                grouped(steps, unknowns),
                whole(slots, steps, window),
                whole(slots * unknowns, unknowns),
                grouped(unknowns, unknowns),
                whole(unknowns, patches),
                whole(patches, unknowns),
                pl.BlockSpec((None, GROUP, patches), lambda g, ids: (g, 0, 0)),
            ],
            out_specs=[grouped(steps, unknowns), grouped(steps, unknowns)],
            scratch_shapes=[
                pltpu.VMEM((3 * per_dev + 1, window, unknowns), jnp.bfloat16),
                pltpu.VMEM((size, slots * unknowns), jnp.bfloat16),
                pltpu.VMEM((size, size), jnp.bfloat16),
                pltpu.SemaphoreType.DMA((6,)),
            ],
        ),
        out_shape=[
            jax.ShapeDtypeStruct(currents.shape, jnp.bfloat16),
            jax.ShapeDtypeStruct(currents.shape, jnp.float32),
        ],
        compiler_params=pltpu.CompilerParams(vmem_limit_bytes=40 << 20),
        cost_estimate=pl.CostEstimate(
            flops=2 * pairs * (window + unknowns), bytes_accessed=8 << 20, transcendentals=0
        ),
    )(
        ids, currents, prev, left, left_prev, right, right_prev, excitation, toep,
        couplings.reshape(slots * unknowns, unknowns), block_inverses, charge_map, potential,
        before.reshape(per_dev // GROUP, GROUP, patches),
    )


def solution(mesh):
    in_specs = (
        P("clus", "tm", None),
        P("clus", "tm", None),
        P("clus", None),
        P(),
        P(),
        P("clus", None, None),
        P(),
        P(),
    )
    out_specs = (P("clus", "tm", None), P("clus", "tm", None))
    return jax.shard_map(
        on_device, mesh=mesh, in_specs=in_specs, out_specs=out_specs, check_vma=False
    )
```

```python
import functools

import jax
import jax.numpy as jnp
from jax import lax
from jax.experimental import pallas as pl
from jax.experimental.pallas import tpu as pltpu
from jax.sharding import PartitionSpec as P

GROUP = 4
PIECES = 4
MESH = pl.DeviceIdType.MESH
LEFT, RIGHT, PREV, LEFT_PREV, RIGHT_PREV = range(5)


def halo_kernel(
    n_tm, n_clus, own_hbm, own, cmap, profile, halo, toep, before, totals,
    send, sib_sem, edge_sem, prev_sem, sib_prev_sem, edge_prev_sem, total_send, total_recv,
):
    i, c = lax.axis_index("tm"), lax.axis_index("clus")
    per_dev, steps, unknowns = own.shape
    slots, _, window = toep.shape
    core = lax.rem(c, 2)
    sibling = c + 1 - 2 * core
    beyond = lax.rem(c + 2 * core - 1 + n_clus, n_clus)
    sib_slot, beyond_slot = 1 - core, core
    wraps = (c == 0) | (c == n_clus - 1)
    piece = per_dev // PIECES

    barrier = pltpu.get_barrier_semaphore()
    for other in (sibling, beyond):
        pl.semaphore_signal(barrier, inc=1, device_id=(i, other), device_id_type=MESH)
    for by in range(1, n_tm):
        pl.semaphore_signal(
            barrier, inc=1, device_id=(lax.rem(i + by, n_tm), c), device_id_type=MESH
        )
    pl.semaphore_wait(barrier, n_tm + 1)

    def remote(src, dst, sent, received, tm, clus):
        return pltpu.make_async_remote_copy(
            src_ref=src, dst_ref=dst, send_sem=sent, recv_sem=received,
            device_id=(tm, clus), device_id_type=MESH,
        )

    later = lax.rem(i + 1, n_tm)

    def rows(j):
        return pl.ds(j * piece, piece)

    def to_edge(j):
        return remote(
            own_hbm.at[rows(j)], halo.at[sib_slot, rows(j)], send.at[0, j], edge_sem.at[j],
            i, beyond,
        )

    def to_later(j):
        return remote(
            own_hbm.at[rows(j)], halo.at[PREV, rows(j)], send.at[1, j], prev_sem.at[j], later, c
        )

    def prev_to_sib(j):
        return remote(
            halo.at[PREV, rows(j)], halo.at[beyond_slot + 3, rows(j)], send.at[2, j],
            sib_prev_sem.at[j], i, sibling,
        )

    def prev_to_edge(j):
        return remote(
            halo.at[PREV, rows(j)], halo.at[sib_slot + 3, rows(j)], send.at[3, j],
            edge_prev_sem.at[j], i, beyond,
        )

    def edge_to_later(j):
        return remote(
            halo.at[beyond_slot, rows(j)], halo.at[beyond_slot + 3, rows(j)], send.at[4, j],
            edge_prev_sem.at[j], later, c,
        )

    to_sib = remote(
        own_hbm, halo.at[beyond_slot], send.at[5, 0], sib_sem.at[0], i, sibling
    )
    has_prev, has_later = i > 0, i < n_tm - 1
    for j in range(PIECES):
        to_edge(j).start()

        @pl.when(has_later)
        def _():
            to_later(j).start()

    to_sib.start()

    sums = jnp.sum(own[...].astype(jnp.float32), axis=1)
    totals[n_tm] = jnp.dot(
        sums, cmap[...].astype(jnp.float32), precision=lax.Precision.HIGHEST,
        preferred_element_type=jnp.float32,
    )

    def total_to(by):
        return remote(
            totals.at[n_tm], totals.at[by], total_send.at[by], total_recv.at[by],
            lax.rem(i + by, n_tm), c,
        )

    for by in range(1, n_tm):

        @pl.when(i + by < n_tm)
        def _():
            total_to(by).start()

    for k in range(slots):
        line = jnp.broadcast_to(profile[pl.ds(k, 1)].astype(jnp.float32), (steps, window))
        toep[k] = pltpu.roll(line, 0, 1, stride=1, stride_axis=0).astype(toep.dtype)

    for j in range(PIECES):

        @pl.when(has_prev)
        def _():
            to_later(j).wait_recv()
            prev_to_sib(j).start()

            @pl.when(jnp.logical_not(wraps))
            def _():
                prev_to_edge(j).start()

        to_edge(j).wait_recv()

        @pl.when(wraps & has_later)
        def _():
            edge_to_later(j).start()

    before[...] = jnp.zeros(before.shape, before.dtype)
    for by in range(1, n_tm):

        @pl.when(i >= by)
        def _():
            total_to(by).wait_recv()
            before[...] += totals[by]

        @pl.when(i + by < n_tm)
        def _():
            total_to(by).wait_send()

    to_sib.wait()
    for j in range(PIECES):
        to_edge(j).wait_send()

        @pl.when(has_later)
        def _():
            to_later(j).wait_send()

        @pl.when(has_prev)
        def _():
            prev_to_sib(j).wait()
            prev_to_edge(j).wait_recv()

        @pl.when(has_prev & jnp.logical_not(wraps))
        def _():
            prev_to_edge(j).wait_send()

        @pl.when(wraps & has_later)
        def _():
            edge_to_later(j).wait_send()


def sweep_kernel(
    ids, early, own, halo, exc, toep, coup, binv, cmap, pot, before,
    upd, res, ext, filt, lower, sems,
):
    group = pl.program_id(0)
    per_dev, steps, unknowns = own.shape
    slots, _, window = toep.shape
    lags = window - steps

    @pl.when(group == 0)
    def _():
        sides = ((LEFT_PREV, halo.at[LEFT]), (PREV, own), (RIGHT_PREV, halo.at[RIGHT]))
        copies, old_copies = [], []
        for n, (old, new) in enumerate(sides):
            place = pl.ds(n * per_dev, per_dev)
            copies.append(
                pltpu.make_async_copy(new, ext.at[place, pl.ds(lags, steps)], sems.at[2 * n])
            )
            old_copies.append(
                pltpu.make_async_copy(
                    halo.at[old], ext.at[place, pl.ds(0, lags)], sems.at[2 * n + 1]
                )
            )
        for copy in copies:
            copy.start()

        @pl.when(early[0] == 0)
        def _():
            for copy in old_copies:
                copy.start()

        @pl.when(early[0] != 0)
        def _():
            ext[:, pl.ds(0, lags)] = jnp.zeros((ext.shape[0], lags, unknowns), ext.dtype)

        ext[3 * per_dev] = jnp.zeros((window, unknowns), ext.dtype)
        size = GROUP * steps
        row = lax.broadcasted_iota(jnp.int32, (size, size), 0)
        col = lax.broadcasted_iota(jnp.int32, (size, size), 1)
        keep = (row >= col) & (row // steps == col // steps)
        lower[...] = jnp.where(keep, 1.0, 0.0).astype(lower.dtype)
        for copy in copies:
            copy.wait()

        @pl.when(early[0] == 0)
        def _():
            for copy in old_copies:
                copy.wait()

    first = group * GROUP
    for k in range(slots):
        for c in range(0, GROUP, 2):
            one = ext[ids[first + c, k]]
            two = ext[ids[first + c + 1, k]]
            both = jnp.concatenate([one, two], axis=1)
            out = jnp.dot(toep[k], both, preferred_element_type=jnp.float32)
            out = out.astype(jnp.bfloat16)
            lanes = pl.ds(k * unknowns, unknowns)
            filt[pl.ds(c * steps, steps), lanes] = out[:, :unknowns]
            filt[pl.ds((c + 1) * steps, steps), lanes] = out[:, unknowns:]
    near = jnp.dot(filt[...], coup[...], preferred_element_type=jnp.float32)

    own_rows = ext[pl.ds(per_dev + first, GROUP), pl.ds(lags, steps)]
    own_rows = own_rows.reshape(GROUP * steps, unknowns)
    incr = jnp.dot(own_rows, cmap[...], preferred_element_type=jnp.float32)
    high = incr.astype(jnp.bfloat16)
    rest = (incr - high.astype(jnp.float32)).astype(jnp.bfloat16)
    sums = jnp.dot(
        lower[...], jnp.concatenate([high, rest], axis=1), preferred_element_type=jnp.float32
    )
    patches = incr.shape[1]
    running = (sums[:, :patches] + sums[:, patches:]).reshape(GROUP, steps, patches)
    charge = (running + before[...][:, None, :]).astype(jnp.bfloat16)
    field = jnp.dot(
        charge.reshape(GROUP * steps, patches), pot[...], preferred_element_type=jnp.float32
    )
    residual = (
        exc[...].astype(jnp.float32).reshape(GROUP * steps, unknowns) - near - field
    )
    res[...] = residual.reshape(GROUP, steps, unknowns)
    rounded = residual.astype(jnp.bfloat16)
    for c in range(GROUP):
        rows = slice(c * steps, (c + 1) * steps)
        step = jnp.dot(rounded[rows], binv[c], preferred_element_type=jnp.float32)
        upd[c] = (own_rows[rows].astype(jnp.float32) + step).astype(upd.dtype)


def on_device(
    currents, excitation, neighbours, lag_profile, couplings, block_inverses, charge_map, potential
):
    per_dev, steps, unknowns = currents.shape
    slots, lags = lag_profile.shape
    window = steps + lags
    patches = charge_map.shape[1]
    n_tm, n_clus = lax.axis_size("tm"), lax.axis_size("clus")
    total = per_dev * n_clus

    vmem = pl.BlockSpec(memory_space=pltpu.VMEM)
    anywhere = pl.BlockSpec(memory_space=pl.ANY)
    profile = jnp.pad(lag_profile[:, ::-1], ((0, 0), (1, window - lags - 1)))
    halo, toep, before = pl.pallas_call(
        functools.partial(halo_kernel, n_tm, n_clus),
        in_specs=[anywhere, vmem, vmem, vmem],
        out_specs=[anywhere, vmem, vmem],
        out_shape=[
            jax.ShapeDtypeStruct((5,) + currents.shape, jnp.bfloat16),
            jax.ShapeDtypeStruct((slots, steps, window), jnp.bfloat16),
            jax.ShapeDtypeStruct((per_dev, patches), jnp.float32),
        ],
        scratch_shapes=[
            pltpu.VMEM((n_tm + 1, per_dev, patches), jnp.float32),
            pltpu.SemaphoreType.DMA((6, PIECES)),
            pltpu.SemaphoreType.DMA((1,)),
            pltpu.SemaphoreType.DMA((PIECES,)),
            pltpu.SemaphoreType.DMA((PIECES,)),
            pltpu.SemaphoreType.DMA((PIECES,)),
            pltpu.SemaphoreType.DMA((PIECES,)),
            pltpu.SemaphoreType.DMA((n_tm,)),
            pltpu.SemaphoreType.DMA((n_tm,)),
        ],
        compiler_params=pltpu.CompilerParams(
            collective_id=0, has_side_effects=True, vmem_limit_bytes=32 << 20
        ),
    )(currents, currents, charge_map, profile)

    first_local = (lax.axis_index("clus") - 1) * per_dev
    ids = jnp.where(neighbours >= 0, (neighbours - first_local) % total, 3 * per_dev)
    early = (lax.axis_index("tm") == 0).astype(jnp.int32).reshape(1)

    def whole(*shape):
        return pl.BlockSpec(shape, lambda g, ids, early: (0,) * len(shape))

    def grouped(*shape):
        return pl.BlockSpec((GROUP,) + shape, lambda g, ids, early: (g,) + (0,) * len(shape))

    size = GROUP * steps
    pairs = per_dev * slots * steps * unknowns
    return pl.pallas_call(
        sweep_kernel,
        grid_spec=pltpu.PrefetchScalarGridSpec(
            num_scalar_prefetch=2,
            grid=(per_dev // GROUP,),
            in_specs=[anywhere] * 2
            + [
                grouped(steps, unknowns),
                whole(slots, steps, window),
                whole(slots * unknowns, unknowns),
                grouped(unknowns, unknowns),
                whole(unknowns, patches),
                whole(patches, unknowns),
                pl.BlockSpec((None, GROUP, patches), lambda g, ids, early: (g, 0, 0)),
            ],
            out_specs=[grouped(steps, unknowns), grouped(steps, unknowns)],
            scratch_shapes=[
                pltpu.VMEM((3 * per_dev + 1, window, unknowns), jnp.bfloat16),
                pltpu.VMEM((size, slots * unknowns), jnp.bfloat16),
                pltpu.VMEM((size, size), jnp.bfloat16),
                pltpu.SemaphoreType.DMA((6,)),
            ],
        ),
        out_shape=[
            jax.ShapeDtypeStruct(currents.shape, jnp.bfloat16),
            jax.ShapeDtypeStruct(currents.shape, jnp.float32),
        ],
        compiler_params=pltpu.CompilerParams(vmem_limit_bytes=40 << 20),
        cost_estimate=pl.CostEstimate(
            flops=2 * pairs * (window + unknowns), bytes_accessed=8 << 20, transcendentals=0
        ),
    )(
        ids, early, currents, halo, excitation, toep,
        couplings.reshape(slots * unknowns, unknowns), block_inverses, charge_map, potential,
        before.reshape(per_dev // GROUP, GROUP, patches),
    )


def solution(mesh):
    in_specs = (
        P("clus", "tm", None),
        P("clus", "tm", None),
        P("clus", None),
        P(),
        P(),
        P("clus", None, None),
        P(),
        P(),
    )
    out_specs = (P("clus", "tm", None), P("clus", "tm", None))
    return jax.shard_map(
        on_device, mesh=mesh, in_specs=in_specs, out_specs=out_specs, check_vma=False
    )
```

```python
import functools

import jax
import jax.numpy as jnp
from jax import lax
from jax.experimental import pallas as pl
from jax.experimental.pallas import tpu as pltpu
from jax.sharding import PartitionSpec as P

GROUP = 4
PIECES = 8
MESH = pl.DeviceIdType.MESH
LEFT, RIGHT, PREV, LEFT_PREV, RIGHT_PREV = range(5)


def halo_kernel(
    n_tm, n_clus, own_hbm, own, cmap, profile, coup, halo, toep, coup_t, before, totals,
    send, sib_sem, edge_sem, prev_sem, sib_prev_sem, edge_prev_sem, total_send, total_recv,
):
    i, c = lax.axis_index("tm"), lax.axis_index("clus")
    per_dev, steps, unknowns = own.shape
    slots, _, window = toep.shape
    core = lax.rem(c, 2)
    sibling = c + 1 - 2 * core
    beyond = lax.rem(c + 2 * core - 1 + n_clus, n_clus)
    sib_slot, beyond_slot = 1 - core, core
    wraps = (c == 0) | (c == n_clus - 1)
    piece = per_dev // PIECES

    barrier = pltpu.get_barrier_semaphore()
    for other in (sibling, beyond):
        pl.semaphore_signal(barrier, inc=1, device_id=(i, other), device_id_type=MESH)
    for by in range(1, n_tm):
        pl.semaphore_signal(
            barrier, inc=1, device_id=(lax.rem(i + by, n_tm), c), device_id_type=MESH
        )
    pl.semaphore_wait(barrier, n_tm + 1)

    def remote(src, dst, sent, received, tm, clus):
        return pltpu.make_async_remote_copy(
            src_ref=src, dst_ref=dst, send_sem=sent, recv_sem=received,
            device_id=(tm, clus), device_id_type=MESH,
        )

    later = lax.rem(i + 1, n_tm)

    def rows(j):
        return pl.ds(j * piece, piece)

    def to_edge(j):
        return remote(
            own_hbm.at[rows(j)], halo.at[sib_slot, rows(j)], send.at[0, j], edge_sem.at[j],
            i, beyond,
        )

    def to_later(j):
        return remote(
            own_hbm.at[rows(j)], halo.at[PREV, rows(j)], send.at[1, j], prev_sem.at[j], later, c
        )

    def prev_to_sib(j):
        return remote(
            halo.at[PREV, rows(j)], halo.at[beyond_slot + 3, rows(j)], send.at[2, j],
            sib_prev_sem.at[j], i, sibling,
        )

    def prev_to_edge(j):
        return remote(
            halo.at[PREV, rows(j)], halo.at[sib_slot + 3, rows(j)], send.at[3, j],
            edge_prev_sem.at[j], i, beyond,
        )

    def edge_to_later(j):
        return remote(
            halo.at[beyond_slot, rows(j)], halo.at[beyond_slot + 3, rows(j)], send.at[4, j],
            edge_prev_sem.at[j], later, c,
        )

    to_sib = remote(
        own_hbm, halo.at[beyond_slot], send.at[5, 0], sib_sem.at[0], i, sibling
    )
    has_prev, has_later = i > 0, i < n_tm - 1
    for j in range(PIECES):
        to_edge(j).start()

        @pl.when(has_later)
        def _():
            to_later(j).start()

    to_sib.start()

    sums = jnp.sum(own[...].astype(jnp.float32), axis=1)
    totals[n_tm] = jnp.dot(
        sums, cmap[...].astype(jnp.float32), precision=lax.Precision.HIGHEST,
        preferred_element_type=jnp.float32,
    )

    def total_to(by):
        return remote(
            totals.at[n_tm], totals.at[by], total_send.at[by], total_recv.at[by],
            lax.rem(i + by, n_tm), c,
        )

    for by in range(1, n_tm):

        @pl.when(i + by < n_tm)
        def _():
            total_to(by).start()

    lags = profile.shape[1]
    lag = lax.broadcasted_iota(jnp.int32, (lags, window), 0)
    place = lax.broadcasted_iota(jnp.int32, (lags, window), 1)
    turn = jnp.where(lag + place == lags, 1.0, 0.0).astype(jnp.bfloat16)
    turned = jnp.dot(profile[...], turn, preferred_element_type=jnp.float32)
    for k in range(slots):
        line = jnp.broadcast_to(turned[k : k + 1], (steps, window))
        toep[k] = pltpu.roll(line, 0, 1, stride=1, stride_axis=0).astype(toep.dtype)
        coup_t[:, pl.ds(k * unknowns, unknowns)] = coup[k].T

    for j in range(PIECES):

        @pl.when(has_prev)
        def _():
            to_later(j).wait_recv()
            prev_to_sib(j).start()

        to_edge(j).wait_recv()

        @pl.when(has_prev & jnp.logical_not(wraps))
        def _():
            prev_to_edge(j).start()

        @pl.when(wraps & has_later)
        def _():
            edge_to_later(j).start()

    before[...] = jnp.zeros(before.shape, before.dtype)
    for by in range(1, n_tm):

        @pl.when(i >= by)
        def _():
            total_to(by).wait_recv()
            before[...] += totals[by]

        @pl.when(i + by < n_tm)
        def _():
            total_to(by).wait_send()

    to_sib.wait()
    for j in range(PIECES):
        to_edge(j).wait_send()

        @pl.when(has_later)
        def _():
            to_later(j).wait_send()

        @pl.when(has_prev)
        def _():
            prev_to_sib(j).wait()
            prev_to_edge(j).wait_recv()

        @pl.when(has_prev & jnp.logical_not(wraps))
        def _():
            prev_to_edge(j).wait_send()

        @pl.when(wraps & has_later)
        def _():
            edge_to_later(j).wait_send()


def sweep_kernel(
    n_clus, neighbours, own, halo, exc, toep, coup_t, binv, cmap, pot, before,
    upd, res, ext, filt, lower, sems,
):
    group = pl.program_id(0)
    has_prev = lax.axis_index("tm") > 0
    first_local = (lax.axis_index("clus") - 1) * own.shape[0]
    total = n_clus * own.shape[0]

    def place_of(cluster, slot):
        at = neighbours[cluster, slot]
        to = at - first_local
        to = jnp.where(to < 0, to + total, to)
        to = jnp.where(to >= total, to - total, to)
        return jnp.where(at < 0, 3 * own.shape[0], to)

    per_dev, steps, unknowns = own.shape
    slots, _, window = toep.shape
    lags = window - steps

    @pl.when(group == 0)
    def _():
        sides = ((LEFT_PREV, halo.at[LEFT]), (PREV, own), (RIGHT_PREV, halo.at[RIGHT]))
        copies, old_copies = [], []
        for n, (old, new) in enumerate(sides):
            place = pl.ds(n * per_dev, per_dev)
            copies.append(
                pltpu.make_async_copy(new, ext.at[place, pl.ds(lags, steps)], sems.at[2 * n])
            )
            old_copies.append(
                pltpu.make_async_copy(
                    halo.at[old], ext.at[place, pl.ds(0, lags)], sems.at[2 * n + 1]
                )
            )
        for copy in copies:
            copy.start()

        @pl.when(has_prev)
        def _():
            for copy in old_copies:
                copy.start()

        @pl.when(jnp.logical_not(has_prev))
        def _():
            ext[:, pl.ds(0, lags)] = jnp.zeros((ext.shape[0], lags, unknowns), ext.dtype)

        ext[3 * per_dev] = jnp.zeros((window, unknowns), ext.dtype)
        size = GROUP * steps
        row = lax.broadcasted_iota(jnp.int32, (size, size), 0)
        col = lax.broadcasted_iota(jnp.int32, (size, size), 1)
        keep = (row >= col) & (row // steps == col // steps)
        lower[...] = jnp.where(keep, 1.0, 0.0).astype(lower.dtype)
        for copy in copies:
            copy.wait()

        @pl.when(has_prev)
        def _():
            for copy in old_copies:
                copy.wait()

    first = group * GROUP
    for k in range(slots):
        for c in range(0, GROUP, 2):
            one = ext[place_of(first + c, k)]
            two = ext[place_of(first + c + 1, k)]
            both = jnp.concatenate([one, two], axis=1)
            out = jnp.dot(toep[k], both, preferred_element_type=jnp.float32)
            out = out.astype(jnp.bfloat16)
            lanes = pl.ds(k * unknowns, unknowns)
            filt[pl.ds(c * steps, steps), lanes] = out[:, :unknowns]
            filt[pl.ds((c + 1) * steps, steps), lanes] = out[:, unknowns:]
    near = lax.dot_general(
        coup_t[...], filt[...], (((1,), (1,)), ((), ())), preferred_element_type=jnp.float32
    ).T

    own_rows = ext[pl.ds(per_dev + first, GROUP), pl.ds(lags, steps)]
    own_rows = own_rows.reshape(GROUP * steps, unknowns)
    incr = jnp.dot(own_rows, cmap[...], preferred_element_type=jnp.float32)
    high = incr.astype(jnp.bfloat16)
    rest = (incr - high.astype(jnp.float32)).astype(jnp.bfloat16)
    sums = jnp.dot(
        lower[...], jnp.concatenate([high, rest], axis=1), preferred_element_type=jnp.float32
    )
    patches = incr.shape[1]
    running = (sums[:, :patches] + sums[:, patches:]).reshape(GROUP, steps, patches)
    charge = (running + before[pl.ds(first, GROUP)][:, None, :]).astype(jnp.bfloat16)
    field = jnp.dot(
        charge.reshape(GROUP * steps, patches), pot[...], preferred_element_type=jnp.float32
    )
    residual = (
        exc[...].astype(jnp.float32).reshape(GROUP * steps, unknowns) - near - field
    )
    res[...] = residual.reshape(GROUP, steps, unknowns)
    rounded = residual.astype(jnp.bfloat16)
    for c in range(GROUP):
        rows = slice(c * steps, (c + 1) * steps)
        step = jnp.dot(rounded[rows], binv[c], preferred_element_type=jnp.float32)
        upd[c] = (own_rows[rows].astype(jnp.float32) + step).astype(upd.dtype)


def on_device(
    currents, excitation, neighbours, lag_profile, couplings, block_inverses, charge_map, potential
):
    per_dev, steps, unknowns = currents.shape
    slots, lags = lag_profile.shape
    window = steps + lags
    patches = charge_map.shape[1]
    n_tm, n_clus = lax.axis_size("tm"), lax.axis_size("clus")

    vmem = pl.BlockSpec(memory_space=pltpu.VMEM)
    anywhere = pl.BlockSpec(memory_space=pl.ANY)
    halo, toep, coup_t, before = pl.pallas_call(
        functools.partial(halo_kernel, n_tm, n_clus),
        in_specs=[anywhere, vmem, vmem, vmem, vmem],
        out_specs=[anywhere, vmem, vmem, vmem],
        out_shape=[
            jax.ShapeDtypeStruct((5,) + currents.shape, jnp.bfloat16),
            jax.ShapeDtypeStruct((slots, steps, window), jnp.bfloat16),
            jax.ShapeDtypeStruct((unknowns, slots * unknowns), jnp.bfloat16),
            jax.ShapeDtypeStruct((per_dev, patches), jnp.float32),
        ],
        scratch_shapes=[
            pltpu.VMEM((n_tm + 1, per_dev, patches), jnp.float32),
            pltpu.SemaphoreType.DMA((6, PIECES)),
            pltpu.SemaphoreType.DMA((1,)),
            pltpu.SemaphoreType.DMA((PIECES,)),
            pltpu.SemaphoreType.DMA((PIECES,)),
            pltpu.SemaphoreType.DMA((PIECES,)),
            pltpu.SemaphoreType.DMA((PIECES,)),
            pltpu.SemaphoreType.DMA((n_tm,)),
            pltpu.SemaphoreType.DMA((n_tm,)),
        ],
        compiler_params=pltpu.CompilerParams(
            collective_id=0, has_side_effects=True, vmem_limit_bytes=56 << 20
        ),
    )(currents, currents, charge_map, lag_profile, couplings)

    def whole(*shape):
        return pl.BlockSpec(shape, lambda g, ids: (0,) * len(shape))

    def grouped(*shape):
        return pl.BlockSpec((GROUP,) + shape, lambda g, ids: (g,) + (0,) * len(shape))

    size = GROUP * steps
    pairs = per_dev * slots * steps * unknowns
    return pl.pallas_call(
        functools.partial(sweep_kernel, n_clus),
        grid_spec=pltpu.PrefetchScalarGridSpec(
            num_scalar_prefetch=1,
            grid=(per_dev // GROUP,),
            in_specs=[anywhere] * 2
            + [
                grouped(steps, unknowns),
                whole(slots, steps, window),
                whole(unknowns, slots * unknowns),
                grouped(unknowns, unknowns),
                whole(unknowns, patches),
                whole(patches, unknowns),
                whole(per_dev, patches),
            ],
            out_specs=[grouped(steps, unknowns), grouped(steps, unknowns)],
            scratch_shapes=[
                pltpu.VMEM((3 * per_dev + 1, window, unknowns), jnp.bfloat16),
                pltpu.VMEM((size, slots * unknowns), jnp.bfloat16),
                pltpu.VMEM((size, size), jnp.bfloat16),
                pltpu.SemaphoreType.DMA((6,)),
            ],
        ),
        out_shape=[
            jax.ShapeDtypeStruct(currents.shape, jnp.bfloat16),
            jax.ShapeDtypeStruct(currents.shape, jnp.float32),
        ],
        compiler_params=pltpu.CompilerParams(vmem_limit_bytes=56 << 20),
        cost_estimate=pl.CostEstimate(
            flops=2 * pairs * (window + unknowns), bytes_accessed=8 << 20, transcendentals=0
        ),
    )(
        neighbours, currents, halo, excitation, toep,
        coup_t, block_inverses, charge_map, potential,
        before,
    )


def solution(mesh):
    in_specs = (
        P("clus", "tm", None),
        P("clus", "tm", None),
        P("clus", None),
        P(),
        P(),
        P("clus", None, None),
        P(),
        P(),
    )
    out_specs = (P("clus", "tm", None), P("clus", "tm", None))
    return jax.shard_map(
        on_device, mesh=mesh, in_specs=in_specs, out_specs=out_specs, check_vma=False
    )
```

```python
import functools

import jax
import jax.numpy as jnp
from jax import lax
from jax.experimental import pallas as pl
from jax.experimental.pallas import tpu as pltpu
from jax.sharding import PartitionSpec as P

GROUP = 4
PIECES = 8
MESH = pl.DeviceIdType.MESH


def sweep_kernel(
    n_tm, n_clus, own_hbm, exc_hbm, coup_hbm, binv_hbm, neighbours, cmap, pot, profile,
    upd_hbm, res_hbm,
    ext, filt, toep, lower, coup, binv, exc, base, upd, res, before, totals,
    send, sib_sem, edge_sem, prev_sem, sib_prev_sem, edge_prev_sem, total_send, total_recv,
    load_sem, store_sem,
):
    i, c = lax.axis_index("tm"), lax.axis_index("clus")
    per_dev, steps, unknowns = own_hbm.shape
    slots, _, window = toep.shape
    lags = profile.shape[1]
    patches = cmap.shape[1]
    groups = per_dev // GROUP
    size = GROUP * steps
    core = lax.rem(c, 2)
    sibling = c + 1 - 2 * core
    beyond = lax.rem(c + 2 * core - 1 + n_clus, n_clus)
    wraps = (c == 0) | (c == n_clus - 1)
    has_prev, has_later = i > 0, i < n_tm - 1
    later = lax.rem(i + 1, n_tm)
    piece = per_dev // PIECES
    from_beyond, from_sibling = 2 * core, 2 - 2 * core

    barrier = pltpu.get_barrier_semaphore()
    for other in (sibling, beyond):
        pl.semaphore_signal(barrier, inc=1, device_id=(i, other), device_id_type=MESH)
    for by in range(1, n_tm):
        pl.semaphore_signal(
            barrier, inc=1, device_id=(lax.rem(i + by, n_tm), c), device_id_type=MESH
        )
    pl.semaphore_wait(barrier, n_tm + 1)

    def remote(src, dst, sent, received, tm, clus):
        return pltpu.make_async_remote_copy(
            src_ref=src, dst_ref=dst, send_sem=sent, recv_sem=received,
            device_id=(tm, clus), device_id_type=MESH,
        )

    def mine(j):
        return own_hbm.at[pl.ds(j * piece, piece)]

    def new(region, j):
        return ext.at[pl.ds(region * per_dev + j * piece, piece), pl.ds(lags, steps)]

    def old(region, j):
        return ext.at[pl.ds(region * per_dev + j * piece, piece), pl.ds(0, lags)]

    def to_edge(j):
        return remote(
            mine(j), new(from_sibling, j), send.at[0, j], edge_sem.at[j], i, beyond
        )

    def to_later(j):
        return remote(mine(j), old(1, j), send.at[1, j], prev_sem.at[j], later, c)

    def prev_to_sib(j):
        return remote(
            old(1, j), old(from_beyond, j), send.at[2, j], sib_prev_sem.at[j], i, sibling
        )

    def prev_to_edge(j):
        return remote(
            old(1, j), old(from_sibling, j), send.at[3, j], edge_prev_sem.at[j], i, beyond
        )

    def edge_to_later(j):
        return remote(
            new(from_beyond, j), old(from_beyond, j), send.at[4, j], edge_prev_sem.at[j],
            later, c,
        )

    to_sib = remote(
        own_hbm, ext.at[pl.ds(from_beyond * per_dev, per_dev), pl.ds(lags, steps)],
        send.at[5, 0], sib_sem.at[0], i, sibling,
    )
    for j in range(PIECES):
        to_edge(j).start()

        @pl.when(has_later)
        def _():
            to_later(j).start()

    to_sib.start()

    own_rows = (pl.ds(per_dev, per_dev), pl.ds(lags, steps))
    load_own = pltpu.make_async_copy(own_hbm, ext.at[own_rows], load_sem.at[0])
    loads = [
        pltpu.make_async_copy(exc_hbm, exc, load_sem.at[1]),
        pltpu.make_async_copy(coup_hbm, coup, load_sem.at[2]),
        pltpu.make_async_copy(binv_hbm, binv, load_sem.at[3]),
    ]
    load_own.start()
    for load in loads:
        load.start()

    ext[3 * per_dev] = jnp.zeros((window, unknowns), ext.dtype)

    @pl.when(jnp.logical_not(has_prev))
    def _():
        ext[pl.ds(0, 3 * per_dev), pl.ds(0, lags)] = jnp.zeros(
            (3 * per_dev, lags, unknowns), ext.dtype
        )

    load_own.wait()
    sums = jnp.sum(ext[own_rows].astype(jnp.float32), axis=1)
    totals[n_tm] = jnp.dot(
        sums, cmap[...].astype(jnp.float32), precision=lax.Precision.HIGHEST,
        preferred_element_type=jnp.float32,
    )

    def total_to(by):
        return remote(
            totals.at[n_tm], totals.at[by], total_send.at[by], total_recv.at[by],
            lax.rem(i + by, n_tm), c,
        )

    for by in range(1, n_tm):

        @pl.when(i + by < n_tm)
        def _():
            total_to(by).start()

    lag = lax.broadcasted_iota(jnp.int32, (lags, window), 0)
    place = lax.broadcasted_iota(jnp.int32, (lags, window), 1)
    turn = jnp.where(lag + place == lags, 1.0, 0.0).astype(jnp.bfloat16)
    turned = jnp.dot(profile[...], turn, preferred_element_type=jnp.float32)
    for k in range(slots):
        line = jnp.broadcast_to(turned[k : k + 1], (steps, window))
        toep[k] = pltpu.roll(line, 0, 1, stride=1, stride_axis=0).astype(toep.dtype)

    row = lax.broadcasted_iota(jnp.int32, (size, size), 0)
    col = lax.broadcasted_iota(jnp.int32, (size, size), 1)
    keep = (row >= col) & (row // steps == col // steps)
    lower[...] = jnp.where(keep, 1.0, 0.0).astype(lower.dtype)

    for j in range(PIECES):

        @pl.when(has_prev)
        def _():
            to_later(j).wait_recv()
            prev_to_sib(j).start()

        to_edge(j).wait_recv()

        @pl.when(has_prev & jnp.logical_not(wraps))
        def _():
            prev_to_edge(j).start()

        @pl.when(wraps & has_later)
        def _():
            edge_to_later(j).start()

    before[...] = jnp.zeros(before.shape, before.dtype)
    for by in range(1, n_tm):

        @pl.when(i >= by)
        def _():
            total_to(by).wait_recv()
            before[...] += totals[by]

    for load in loads:
        load.wait()

    def charge_group(group, carry):
        first = group * GROUP
        rows = ext[pl.ds(per_dev + first, GROUP), pl.ds(lags, steps)].reshape(size, unknowns)
        incr = jnp.dot(rows, cmap[...], preferred_element_type=jnp.float32)
        high = incr.astype(jnp.bfloat16)
        rest = (incr - high.astype(jnp.float32)).astype(jnp.bfloat16)
        sums = jnp.dot(
            lower[...], jnp.concatenate([high, rest], axis=1), preferred_element_type=jnp.float32
        )
        running = (sums[:, :patches] + sums[:, patches:]).reshape(GROUP, steps, patches)
        charge = (running + before[pl.ds(first, GROUP)][:, None, :]).astype(jnp.bfloat16)
        field = jnp.dot(
            charge.reshape(size, patches), pot[...], preferred_element_type=jnp.float32
        )
        field = field.reshape(GROUP, steps, unknowns)
        place = pl.ds(first, GROUP)
        base[place] = exc[place].astype(jnp.float32) - field
        return carry

    lax.fori_loop(0, groups, charge_group, 0)

    to_sib.wait_recv()
    for j in range(PIECES):

        @pl.when(has_prev)
        def _():
            prev_to_sib(j).wait_recv()
            prev_to_edge(j).wait_recv()

    first_local = (c - 1) * per_dev
    total = per_dev * n_clus

    def place_of(cluster, slot):
        at = neighbours[cluster, slot]
        if total & (total - 1) == 0:
            to = (at - first_local) & (total - 1)
        else:
            to = lax.rem(at - first_local + total, total)
        return jnp.where(at < 0, 3 * per_dev, jnp.minimum(to, 3 * per_dev))

    def stores(group):
        place = pl.ds(group * GROUP, GROUP)
        return (
            pltpu.make_async_copy(res.at[place], res_hbm.at[place], store_sem.at[0, group]),
            pltpu.make_async_copy(upd.at[place], upd_hbm.at[place], store_sem.at[1, group]),
        )

    def sweep_group(group, carry):
        first = group * GROUP
        for k in range(slots):
            for n in range(0, GROUP, 2):
                one = ext[place_of(first + n, k)]
                two = ext[place_of(first + n + 1, k)]
                both = jnp.concatenate([one, two], axis=1)
                out = jnp.dot(toep[k], both, preferred_element_type=jnp.float32)
                out = out.astype(jnp.bfloat16)
                lanes = pl.ds(k * unknowns, unknowns)
                filt[pl.ds(n * steps, steps), lanes] = out[:, :unknowns]
                filt[pl.ds((n + 1) * steps, steps), lanes] = out[:, unknowns:]
        near = jnp.dot(filt[...], coup[...], preferred_element_type=jnp.float32)
        place = pl.ds(first, GROUP)
        residual = base[place] - near.reshape(GROUP, steps, unknowns)
        res[place] = residual
        rounded = residual.astype(jnp.bfloat16)
        rows = ext[pl.ds(per_dev + first, GROUP), pl.ds(lags, steps)]
        for n in range(GROUP):
            step = jnp.dot(rounded[n], binv[first + n], preferred_element_type=jnp.float32)
            upd[first + n] = (rows[n].astype(jnp.float32) + step).astype(upd.dtype)
        for store in stores(group):
            store.start()
        return carry

    lax.fori_loop(0, groups, sweep_group, 0)

    to_sib.wait_send()
    for by in range(1, n_tm):

        @pl.when(i + by < n_tm)
        def _():
            total_to(by).wait_send()

    for j in range(PIECES):
        to_edge(j).wait_send()

        @pl.when(has_later)
        def _():
            to_later(j).wait_send()

        @pl.when(has_prev)
        def _():
            prev_to_sib(j).wait_send()

        @pl.when(has_prev & jnp.logical_not(wraps))
        def _():
            prev_to_edge(j).wait_send()

        @pl.when(wraps & has_later)
        def _():
            edge_to_later(j).wait_send()

    for group in range(groups):
        for store in stores(group):
            store.wait()


def on_device(
    currents, excitation, neighbours, lag_profile, couplings, block_inverses, charge_map, potential
):
    per_dev, steps, unknowns = currents.shape
    slots, lags = lag_profile.shape
    window = steps + lags
    patches = charge_map.shape[1]
    n_tm, n_clus = lax.axis_size("tm"), lax.axis_size("clus")
    vmem = pl.BlockSpec(memory_space=pltpu.VMEM)
    smem = pl.BlockSpec(memory_space=pltpu.SMEM)
    anywhere = pl.BlockSpec(memory_space=pl.ANY)
    size = GROUP * steps
    pairs = per_dev * slots * steps * unknowns
    bf16, f32 = jnp.bfloat16, jnp.float32
    return pl.pallas_call(
        functools.partial(sweep_kernel, n_tm, n_clus),
        in_specs=[anywhere] * 4 + [smem, vmem, vmem, vmem],
        out_specs=[anywhere, anywhere],
        out_shape=[
            jax.ShapeDtypeStruct(currents.shape, bf16),
            jax.ShapeDtypeStruct(currents.shape, f32),
        ],
        scratch_shapes=[
            pltpu.VMEM((3 * per_dev + 1, window, unknowns), bf16),
            pltpu.VMEM((size, slots * unknowns), bf16),
            pltpu.VMEM((slots, steps, window), bf16),
            pltpu.VMEM((size, size), bf16),
            pltpu.VMEM((slots * unknowns, unknowns), bf16),
            pltpu.VMEM(block_inverses.shape, bf16),
            pltpu.VMEM(excitation.shape, bf16),
            pltpu.VMEM(currents.shape, f32),
            pltpu.VMEM(currents.shape, bf16),
            pltpu.VMEM(currents.shape, f32),
            pltpu.VMEM((per_dev, patches), f32),
            pltpu.VMEM((n_tm + 1, per_dev, patches), f32),
            pltpu.SemaphoreType.DMA((6, PIECES)),
            pltpu.SemaphoreType.DMA((1,)),
            pltpu.SemaphoreType.DMA((PIECES,)),
            pltpu.SemaphoreType.DMA((PIECES,)),
            pltpu.SemaphoreType.DMA((PIECES,)),
            pltpu.SemaphoreType.DMA((PIECES,)),
            pltpu.SemaphoreType.DMA((n_tm,)),
            pltpu.SemaphoreType.DMA((n_tm,)),
            pltpu.SemaphoreType.DMA((4,)),
            pltpu.SemaphoreType.DMA((2, per_dev // GROUP)),
        ],
        compiler_params=pltpu.CompilerParams(
            collective_id=0, has_side_effects=True, vmem_limit_bytes=56 << 20
        ),
        cost_estimate=pl.CostEstimate(
            flops=2 * pairs * (window + unknowns), bytes_accessed=8 << 20, transcendentals=0
        ),
    )(
        currents, excitation, couplings.reshape(slots * unknowns, unknowns), block_inverses,
        neighbours, charge_map, potential, lag_profile,
    )


def solution(mesh):
    in_specs = (
        P("clus", "tm", None),
        P("clus", "tm", None),
        P("clus", None),
        P(),
        P(),
        P("clus", None, None),
        P(),
        P(),
    )
    out_specs = (P("clus", "tm", None), P("clus", "tm", None))
    return jax.shard_map(
        on_device, mesh=mesh, in_specs=in_specs, out_specs=out_specs, check_vma=False
    )
```

```python
import functools

import jax
import jax.numpy as jnp
from jax import lax
from jax.experimental import pallas as pl
from jax.experimental.pallas import tpu as pltpu
from jax.sharding import PartitionSpec as P

GROUP = 8
CHARGE_GROUP = 4
PIECES = 8
MESH = pl.DeviceIdType.MESH


def sweep_kernel(
    n_tm, n_clus, own_hbm, exc_hbm, coup_hbm, binv_hbm, neighbours, cmap, pot, profile,
    corr_hbm, fields_hbm,
    ext, filt, toep, lower, coup, binv, exc, base, corr, fields, before, totals,
    send, sib_sem, edge_sem, prev_sem, sib_prev_sem, edge_prev_sem, total_send, total_recv,
    load_sem, store_sem,
):
    i, c = lax.axis_index("tm"), lax.axis_index("clus")
    per_dev, steps, unknowns = own_hbm.shape
    slots, _, window = toep.shape
    lags = profile.shape[1]
    patches = cmap.shape[1]
    groups = per_dev // GROUP
    size = CHARGE_GROUP * steps
    core = lax.rem(c, 2)
    sibling = c + 1 - 2 * core
    beyond = lax.rem(c + 2 * core - 1 + n_clus, n_clus)
    wraps = (c == 0) | (c == n_clus - 1)
    has_prev, has_later = i > 0, i < n_tm - 1
    later = lax.rem(i + 1, n_tm)
    piece = per_dev // PIECES
    even = lax.rem(i, 2) == 0

    def wrap_over_tm(j):
        return wraps & has_later & (even | (j < PIECES // 2))

    def prev_over_clus(j):
        return has_prev & (jnp.logical_not(wraps) | (even & (j >= PIECES // 2)))

    from_beyond, from_sibling = 2 * core, 2 - 2 * core

    barrier = pltpu.get_barrier_semaphore()
    for other in (sibling, beyond):
        pl.semaphore_signal(barrier, inc=1, device_id=(i, other), device_id_type=MESH)
    for by in range(1, n_tm):
        pl.semaphore_signal(
            barrier, inc=1, device_id=(lax.rem(i + by, n_tm), c), device_id_type=MESH
        )
    pl.semaphore_wait(barrier, n_tm + 1)

    def remote(src, dst, sent, received, tm, clus):
        return pltpu.make_async_remote_copy(
            src_ref=src, dst_ref=dst, send_sem=sent, recv_sem=received,
            device_id=(tm, clus), device_id_type=MESH,
        )

    def mine(j):
        return own_hbm.at[pl.ds(j * piece, piece)]

    def new(region, j):
        return ext.at[pl.ds(region * per_dev + j * piece, piece), pl.ds(lags, steps)]

    def old(region, j):
        return ext.at[pl.ds(region * per_dev + j * piece, piece), pl.ds(0, lags)]

    def to_edge(j):
        return remote(
            mine(j), new(from_sibling, j), send.at[0, j], edge_sem.at[j], i, beyond
        )

    def to_later(j):
        return remote(mine(j), old(1, j), send.at[1, j], prev_sem.at[j], later, c)

    def prev_to_sib(j):
        return remote(
            old(1, j), old(from_beyond, j), send.at[2, j], sib_prev_sem.at[j], i, sibling
        )

    def prev_to_edge(j):
        return remote(
            old(1, j), old(from_sibling, j), send.at[3, j], edge_prev_sem.at[j], i, beyond
        )

    def edge_to_later(j):
        return remote(
            new(from_beyond, j), old(from_beyond, j), send.at[4, j], edge_prev_sem.at[j],
            later, c,
        )

    to_sib = remote(
        own_hbm, ext.at[pl.ds(from_beyond * per_dev, per_dev), pl.ds(lags, steps)],
        send.at[5, 0], sib_sem.at[0], i, sibling,
    )
    for j in range(PIECES):
        to_edge(j).start()

        @pl.when(has_later)
        def _():
            to_later(j).start()

    to_sib.start()

    own_rows = (pl.ds(per_dev, per_dev), pl.ds(lags, steps))
    load_own = pltpu.make_async_copy(own_hbm, ext.at[own_rows], load_sem.at[0])
    loads = [
        pltpu.make_async_copy(exc_hbm, exc, load_sem.at[1]),
        pltpu.make_async_copy(coup_hbm, coup, load_sem.at[2]),
        pltpu.make_async_copy(binv_hbm, binv, load_sem.at[3]),
    ]
    load_own.start()
    for load in loads:
        load.start()

    ext[3 * per_dev] = jnp.zeros((window, unknowns), ext.dtype)

    @pl.when(jnp.logical_not(has_prev))
    def _():
        ext[pl.ds(0, 3 * per_dev), pl.ds(0, lags)] = jnp.zeros(
            (3 * per_dev, lags, unknowns), ext.dtype
        )

    load_own.wait()
    sums = jnp.sum(ext[own_rows].astype(jnp.float32), axis=1)
    totals[n_tm] = jnp.dot(
        sums, cmap[...].astype(jnp.float32), precision=lax.Precision.HIGHEST,
        preferred_element_type=jnp.float32,
    )

    def total_to(by):
        return remote(
            totals.at[n_tm], totals.at[by], total_send.at[by], total_recv.at[by],
            lax.rem(i + by, n_tm), c,
        )

    for by in range(1, n_tm):

        @pl.when(i + by < n_tm)
        def _():
            total_to(by).start()

    lag = lax.broadcasted_iota(jnp.int32, (lags, window), 0)
    place = lax.broadcasted_iota(jnp.int32, (lags, window), 1)
    turn = jnp.where(lag + place == lags, 1.0, 0.0).astype(jnp.bfloat16)
    turned = jnp.dot(profile[...], turn, preferred_element_type=jnp.float32)
    for k in range(slots):
        line = jnp.broadcast_to(turned[k : k + 1], (steps, window))
        toep[k] = pltpu.roll(line, 0, 1, stride=1, stride_axis=0).astype(toep.dtype)

    row = lax.broadcasted_iota(jnp.int32, (size, size), 0)
    col = lax.broadcasted_iota(jnp.int32, (size, size), 1)
    keep = (row >= col) & (row // steps == col // steps)
    lower[...] = jnp.where(keep, 1.0, 0.0).astype(lower.dtype)

    for j in range(PIECES):

        @pl.when(has_prev)
        def _():
            to_later(j).wait_recv()
            prev_to_sib(j).start()

        to_edge(j).wait_recv()

        @pl.when(prev_over_clus(j))
        def _():
            prev_to_edge(j).start()

        @pl.when(wrap_over_tm(j))
        def _():
            edge_to_later(j).start()

    before[...] = jnp.zeros(before.shape, before.dtype)
    for by in range(1, n_tm):

        @pl.when(i >= by)
        def _():
            total_to(by).wait_recv()
            before[...] += totals[by]

    for load in loads:
        load.wait()

    def charge_group(group, carry):
        first = group * CHARGE_GROUP
        rows = ext[pl.ds(per_dev + first, CHARGE_GROUP), pl.ds(lags, steps)].reshape(size, unknowns)
        incr = jnp.dot(rows, cmap[...], preferred_element_type=jnp.float32)
        high = incr.astype(jnp.bfloat16)
        rest = (incr - high.astype(jnp.float32)).astype(jnp.bfloat16)
        sums = jnp.dot(
            lower[...], jnp.concatenate([high, rest], axis=1), preferred_element_type=jnp.float32
        )
        running = (sums[:, :patches] + sums[:, patches:]).reshape(CHARGE_GROUP, steps, patches)
        charge = (running + before[pl.ds(first, CHARGE_GROUP)][:, None, :]).astype(jnp.bfloat16)
        field = jnp.dot(
            charge.reshape(size, patches), pot[...], preferred_element_type=jnp.float32
        )
        base[pl.ds(first, CHARGE_GROUP)] = field.reshape(CHARGE_GROUP, steps, unknowns)
        return carry

    lax.fori_loop(0, per_dev // CHARGE_GROUP, charge_group, 0)

    to_sib.wait_recv()
    for j in range(PIECES):

        @pl.when(has_prev)
        def _():
            prev_to_sib(j).wait_recv()
            prev_to_edge(j).wait_recv()

    first_local = (c - 1) * per_dev
    total = per_dev * n_clus

    def place_of(cluster, slot):
        at = neighbours[cluster, slot]
        if total & (total - 1) == 0:
            to = (at - first_local) & (total - 1)
        else:
            to = lax.rem(at - first_local + total, total)
        return jnp.where(at < 0, 3 * per_dev, jnp.minimum(to, 3 * per_dev))

    def stores(group):
        place = pl.ds(group * GROUP, GROUP)
        return (
            pltpu.make_async_copy(fields.at[place], fields_hbm.at[place], store_sem.at[0, group]),
            pltpu.make_async_copy(corr.at[place], corr_hbm.at[place], store_sem.at[1, group]),
        )

    def sweep_group(group, carry):
        first = group * GROUP
        for k in range(slots):
            for n in range(0, GROUP, 2):
                one = ext[place_of(first + n, k)]
                two = ext[place_of(first + n + 1, k)]
                both = jnp.concatenate([one, two], axis=1)
                out = jnp.dot(toep[k], both, preferred_element_type=jnp.float32)
                out = out.astype(jnp.bfloat16)
                lanes = pl.ds(k * unknowns, unknowns)
                filt[pl.ds(n * steps, steps), lanes] = out[:, :unknowns]
                filt[pl.ds((n + 1) * steps, steps), lanes] = out[:, unknowns:]
        near = jnp.dot(filt[...], coup[...], preferred_element_type=jnp.float32)
        place = pl.ds(first, GROUP)
        both_fields = base[place] + near.reshape(GROUP, steps, unknowns)
        fields[place] = both_fields
        rounded = (exc[place].astype(jnp.float32) - both_fields).astype(jnp.bfloat16)
        for n in range(GROUP):
            corr[first + n] = jnp.dot(
                rounded[n], binv[first + n], preferred_element_type=jnp.float32
            )
        for store in stores(group):
            store.start()
        return carry

    lax.fori_loop(0, groups, sweep_group, 0)

    to_sib.wait_send()
    for by in range(1, n_tm):

        @pl.when(i + by < n_tm)
        def _():
            total_to(by).wait_send()

    for j in range(PIECES):
        to_edge(j).wait_send()

        @pl.when(has_later)
        def _():
            to_later(j).wait_send()

        @pl.when(has_prev)
        def _():
            prev_to_sib(j).wait_send()

        @pl.when(prev_over_clus(j))
        def _():
            prev_to_edge(j).wait_send()

        @pl.when(wrap_over_tm(j))
        def _():
            edge_to_later(j).wait_send()

    for group in range(groups):
        for store in stores(group):
            store.wait()


def on_device(
    currents, excitation, neighbours, lag_profile, couplings, block_inverses, charge_map, potential
):
    per_dev, steps, unknowns = currents.shape
    slots, lags = lag_profile.shape
    window = steps + lags
    patches = charge_map.shape[1]
    n_tm, n_clus = lax.axis_size("tm"), lax.axis_size("clus")
    vmem = pl.BlockSpec(memory_space=pltpu.VMEM)
    smem = pl.BlockSpec(memory_space=pltpu.SMEM)
    anywhere = pl.BlockSpec(memory_space=pl.ANY)
    size = CHARGE_GROUP * steps
    pairs = per_dev * slots * steps * unknowns
    bf16, f32 = jnp.bfloat16, jnp.float32
    correction, fields = pl.pallas_call(
        functools.partial(sweep_kernel, n_tm, n_clus),
        in_specs=[anywhere] * 4 + [smem, vmem, vmem, vmem],
        out_specs=[anywhere, anywhere],
        out_shape=[
            jax.ShapeDtypeStruct(currents.shape, f32),
            jax.ShapeDtypeStruct(currents.shape, f32),
        ],
        scratch_shapes=[
            pltpu.VMEM((3 * per_dev + 1, window, unknowns), bf16),
            pltpu.VMEM((GROUP * steps, slots * unknowns), bf16),
            pltpu.VMEM((slots, steps, window), bf16),
            pltpu.VMEM((size, size), bf16),
            pltpu.VMEM((slots * unknowns, unknowns), bf16),
            pltpu.VMEM(block_inverses.shape, bf16),
            pltpu.VMEM(excitation.shape, bf16),
            pltpu.VMEM(currents.shape, f32),
            pltpu.VMEM(currents.shape, f32),
            pltpu.VMEM(currents.shape, f32),
            pltpu.VMEM((per_dev, patches), f32),
            pltpu.VMEM((n_tm + 1, per_dev, patches), f32),
            pltpu.SemaphoreType.DMA((6, PIECES)),
            pltpu.SemaphoreType.DMA((1,)),
            pltpu.SemaphoreType.DMA((PIECES,)),
            pltpu.SemaphoreType.DMA((PIECES,)),
            pltpu.SemaphoreType.DMA((PIECES,)),
            pltpu.SemaphoreType.DMA((PIECES,)),
            pltpu.SemaphoreType.DMA((n_tm,)),
            pltpu.SemaphoreType.DMA((n_tm,)),
            pltpu.SemaphoreType.DMA((4,)),
            pltpu.SemaphoreType.DMA((2, per_dev // GROUP)),
        ],
        compiler_params=pltpu.CompilerParams(
            collective_id=0, has_side_effects=True, vmem_limit_bytes=56 << 20
        ),
        cost_estimate=pl.CostEstimate(
            flops=2 * pairs * (window + unknowns), bytes_accessed=8 << 20, transcendentals=0
        ),
    )(
        currents, excitation, couplings.reshape(slots * unknowns, unknowns), block_inverses,
        neighbours, charge_map, potential, lag_profile,
    )
    residual = excitation.astype(f32) - fields
    updated = (currents.astype(f32) + correction).astype(bf16)
    return (updated, residual)


def solution(mesh):
    in_specs = (
        P("clus", "tm", None),
        P("clus", "tm", None),
        P("clus", None),
        P(),
        P(),
        P("clus", None, None),
        P(),
        P(),
    )
    out_specs = (P("clus", "tm", None), P("clus", "tm", None))
    return jax.shard_map(
        on_device, mesh=mesh, in_specs=in_specs, out_specs=out_specs, check_vma=False
    )
```

```python
import functools

import jax
import jax.numpy as jnp
from jax import lax
from jax.experimental import pallas as pl
from jax.experimental.pallas import tpu as pltpu
from jax.sharding import PartitionSpec as P

GROUP = 8
CHARGE_GROUP = 4
PIECES = 8
MESH = pl.DeviceIdType.MESH


def sweep_kernel(
    n_tm, n_clus, own_hbm, exc_hbm, coup_hbm, binv_hbm, neighbours, cmap, pot, profile,
    corr, fields,
    ext, filt, toep, lower, coup, binv, exc, base, before, totals,
    send, sib_sem, edge_sem, prev_sem, sib_prev_sem, edge_prev_sem, total_send, total_recv,
    load_sem,
):
    i, c = lax.axis_index("tm"), lax.axis_index("clus")
    per_dev, steps, unknowns = own_hbm.shape
    slots, _, window = toep.shape
    lags = profile.shape[1]
    patches = cmap.shape[1]
    groups = per_dev // GROUP
    size = CHARGE_GROUP * steps
    core = lax.rem(c, 2)
    sibling = c + 1 - 2 * core
    beyond = lax.rem(c + 2 * core - 1 + n_clus, n_clus)
    wraps = (c == 0) | (c == n_clus - 1)
    has_prev, has_later = i > 0, i < n_tm - 1
    later = lax.rem(i + 1, n_tm)
    piece = per_dev // PIECES
    even = lax.rem(i, 2) == 0

    def wrap_over_tm(j):
        return wraps & has_later & (even | (j < 5 * PIECES // 8))

    def prev_over_clus(j):
        return has_prev & (jnp.logical_not(wraps) | (even & (j >= 5 * PIECES // 8)))

    from_beyond, from_sibling = 2 * core, 2 - 2 * core

    barrier = pltpu.get_barrier_semaphore()
    for other in (sibling, beyond):
        pl.semaphore_signal(barrier, inc=1, device_id=(i, other), device_id_type=MESH)
    for by in range(1, n_tm):
        pl.semaphore_signal(
            barrier, inc=1, device_id=(lax.rem(i + by, n_tm), c), device_id_type=MESH
        )
    pl.semaphore_wait(barrier, n_tm + 1)

    def remote(src, dst, sent, received, tm, clus):
        return pltpu.make_async_remote_copy(
            src_ref=src, dst_ref=dst, send_sem=sent, recv_sem=received,
            device_id=(tm, clus), device_id_type=MESH,
        )

    def mine(j):
        return own_hbm.at[pl.ds(j * piece, piece)]

    def new(region, j):
        return ext.at[pl.ds(region * per_dev + j * piece, piece), pl.ds(lags, steps)]

    def old(region, j):
        return ext.at[pl.ds(region * per_dev + j * piece, piece), pl.ds(0, lags)]

    def to_edge(j):
        return remote(
            mine(j), new(from_sibling, j), send.at[0, j], edge_sem.at[j], i, beyond
        )

    def to_later(j):
        return remote(mine(j), old(1, j), send.at[1, j], prev_sem.at[j], later, c)

    def prev_to_sib(j):
        return remote(
            old(1, j), old(from_beyond, j), send.at[2, j], sib_prev_sem.at[j], i, sibling
        )

    def prev_to_edge(j):
        return remote(
            old(1, j), old(from_sibling, j), send.at[3, j], edge_prev_sem.at[j], i, beyond
        )

    def edge_to_later(j):
        return remote(
            new(from_beyond, j), old(from_beyond, j), send.at[4, j], edge_prev_sem.at[j],
            later, c,
        )

    to_sib = remote(
        own_hbm, ext.at[pl.ds(from_beyond * per_dev, per_dev), pl.ds(lags, steps)],
        send.at[5, 0], sib_sem.at[0], i, sibling,
    )
    for j in range(PIECES):
        to_edge(j).start()

        @pl.when(has_later)
        def _():
            to_later(j).start()

    to_sib.start()

    own_rows = (pl.ds(per_dev, per_dev), pl.ds(lags, steps))
    load_own = pltpu.make_async_copy(own_hbm, ext.at[own_rows], load_sem.at[0])
    loads = [
        pltpu.make_async_copy(exc_hbm, exc, load_sem.at[1]),
        pltpu.make_async_copy(coup_hbm, coup, load_sem.at[2]),
        pltpu.make_async_copy(binv_hbm, binv, load_sem.at[3]),
    ]
    load_own.start()
    for load in loads:
        load.start()

    ext[3 * per_dev] = jnp.zeros((window, unknowns), ext.dtype)

    @pl.when(jnp.logical_not(has_prev))
    def _():
        ext[pl.ds(0, 3 * per_dev), pl.ds(0, lags)] = jnp.zeros(
            (3 * per_dev, lags, unknowns), ext.dtype
        )

    load_own.wait()
    sums = jnp.sum(ext[own_rows].astype(jnp.float32), axis=1)
    totals[n_tm] = jnp.dot(
        sums, cmap[...].astype(jnp.float32), precision=lax.Precision.HIGHEST,
        preferred_element_type=jnp.float32,
    )

    def total_to(by):
        return remote(
            totals.at[n_tm], totals.at[by], total_send.at[by], total_recv.at[by],
            lax.rem(i + by, n_tm), c,
        )

    for by in range(1, n_tm):

        @pl.when(i + by < n_tm)
        def _():
            total_to(by).start()

    lag = lax.broadcasted_iota(jnp.int32, (lags, window), 0)
    place = lax.broadcasted_iota(jnp.int32, (lags, window), 1)
    turn = jnp.where(lag + place == lags, 1.0, 0.0).astype(jnp.bfloat16)
    turned = jnp.dot(profile[...], turn, preferred_element_type=jnp.float32)
    for k in range(slots):
        line = jnp.broadcast_to(turned[k : k + 1], (steps, window))
        toep[k] = pltpu.roll(line, 0, 1, stride=1, stride_axis=0).astype(toep.dtype)

    row = lax.broadcasted_iota(jnp.int32, (size, size), 0)
    col = lax.broadcasted_iota(jnp.int32, (size, size), 1)
    keep = (row >= col) & (row // steps == col // steps)
    lower[...] = jnp.where(keep, 1.0, 0.0).astype(lower.dtype)

    for j in range(PIECES):

        @pl.when(has_prev)
        def _():
            to_later(j).wait_recv()
            prev_to_sib(j).start()

        to_edge(j).wait_recv()

        @pl.when(prev_over_clus(j))
        def _():
            prev_to_edge(j).start()

        @pl.when(wrap_over_tm(j))
        def _():
            edge_to_later(j).start()

    before[...] = jnp.zeros(before.shape, before.dtype)
    for by in range(1, n_tm):

        @pl.when(i >= by)
        def _():
            total_to(by).wait_recv()
            before[...] += totals[by]

    for load in loads:
        load.wait()

    def charge_group(group, carry):
        first = group * CHARGE_GROUP
        rows = ext[pl.ds(per_dev + first, CHARGE_GROUP), pl.ds(lags, steps)].reshape(size, unknowns)
        incr = jnp.dot(rows, cmap[...], preferred_element_type=jnp.float32)
        high = incr.astype(jnp.bfloat16)
        rest = (incr - high.astype(jnp.float32)).astype(jnp.bfloat16)
        sums = jnp.dot(
            lower[...], jnp.concatenate([high, rest], axis=1), preferred_element_type=jnp.float32
        )
        running = (sums[:, :patches] + sums[:, patches:]).reshape(CHARGE_GROUP, steps, patches)
        charge = (running + before[pl.ds(first, CHARGE_GROUP)][:, None, :]).astype(jnp.bfloat16)
        field = jnp.dot(
            charge.reshape(size, patches), pot[...], preferred_element_type=jnp.float32
        )
        base[pl.ds(first, CHARGE_GROUP)] = field.reshape(CHARGE_GROUP, steps, unknowns)
        return carry

    lax.fori_loop(0, per_dev // CHARGE_GROUP, charge_group, 0)

    to_sib.wait_recv()
    for j in range(PIECES):

        @pl.when(has_prev)
        def _():
            prev_to_sib(j).wait_recv()
            prev_to_edge(j).wait_recv()

    first_local = (c - 1) * per_dev
    total = per_dev * n_clus

    def place_of(cluster, slot):
        at = neighbours[cluster, slot]
        if total & (total - 1) == 0:
            to = (at - first_local) & (total - 1)
        else:
            to = lax.rem(at - first_local + total, total)
        return jnp.where(at < 0, 3 * per_dev, jnp.minimum(to, 3 * per_dev))

    def sweep_group(group, carry):
        first = group * GROUP
        for k in range(slots):
            for n in range(0, GROUP, 2):
                one = ext[place_of(first + n, k)]
                two = ext[place_of(first + n + 1, k)]
                both = jnp.concatenate([one, two], axis=1)
                out = jnp.dot(toep[k], both, preferred_element_type=jnp.float32)
                out = out.astype(jnp.bfloat16)
                lanes = pl.ds(k * unknowns, unknowns)
                filt[pl.ds(n * steps, steps), lanes] = out[:, :unknowns]
                filt[pl.ds((n + 1) * steps, steps), lanes] = out[:, unknowns:]
        near = jnp.dot(filt[...], coup[...], preferred_element_type=jnp.float32)
        place = pl.ds(first, GROUP)
        both_fields = base[place] + near.reshape(GROUP, steps, unknowns)
        fields[place] = both_fields
        rounded = (exc[place].astype(jnp.float32) - both_fields).astype(jnp.bfloat16)
        for n in range(GROUP):
            corr[first + n] = jnp.dot(
                rounded[n], binv[first + n], preferred_element_type=jnp.float32
            )
        return carry

    lax.fori_loop(0, groups, sweep_group, 0)

    to_sib.wait_send()
    for by in range(1, n_tm):

        @pl.when(i + by < n_tm)
        def _():
            total_to(by).wait_send()

    for j in range(PIECES):
        to_edge(j).wait_send()

        @pl.when(has_later)
        def _():
            to_later(j).wait_send()

        @pl.when(has_prev)
        def _():
            prev_to_sib(j).wait_send()

        @pl.when(prev_over_clus(j))
        def _():
            prev_to_edge(j).wait_send()

        @pl.when(wrap_over_tm(j))
        def _():
            edge_to_later(j).wait_send()


def on_device(
    currents, excitation, neighbours, lag_profile, couplings, block_inverses, charge_map, potential
):
    per_dev, steps, unknowns = currents.shape
    slots, lags = lag_profile.shape
    window = steps + lags
    patches = charge_map.shape[1]
    n_tm, n_clus = lax.axis_size("tm"), lax.axis_size("clus")
    vmem = pl.BlockSpec(memory_space=pltpu.VMEM)
    smem = pl.BlockSpec(memory_space=pltpu.SMEM)
    hbm = pl.BlockSpec(memory_space=pltpu.HBM)
    size = CHARGE_GROUP * steps
    pairs = per_dev * slots * steps * unknowns
    bf16, f32 = jnp.bfloat16, jnp.float32
    correction, fields = pl.pallas_call(
        functools.partial(sweep_kernel, n_tm, n_clus),
        in_specs=[hbm] * 4 + [smem, vmem, vmem, vmem],
        out_specs=[vmem, vmem],
        out_shape=[
            pltpu.VMEM(currents.shape, f32),
            pltpu.VMEM(currents.shape, f32),
        ],
        scratch_shapes=[
            pltpu.VMEM((3 * per_dev + 1, window, unknowns), bf16),
            pltpu.VMEM((GROUP * steps, slots * unknowns), bf16),
            pltpu.VMEM((slots, steps, window), bf16),
            pltpu.VMEM((size, size), bf16),
            pltpu.VMEM((slots * unknowns, unknowns), bf16),
            pltpu.VMEM(block_inverses.shape, bf16),
            pltpu.VMEM(excitation.shape, bf16),
            pltpu.VMEM(currents.shape, f32),
            pltpu.VMEM((per_dev, patches), f32),
            pltpu.VMEM((n_tm + 1, per_dev, patches), f32),
            pltpu.SemaphoreType.DMA((6, PIECES)),
            pltpu.SemaphoreType.DMA((1,)),
            pltpu.SemaphoreType.DMA((PIECES,)),
            pltpu.SemaphoreType.DMA((PIECES,)),
            pltpu.SemaphoreType.DMA((PIECES,)),
            pltpu.SemaphoreType.DMA((PIECES,)),
            pltpu.SemaphoreType.DMA((n_tm,)),
            pltpu.SemaphoreType.DMA((n_tm,)),
            pltpu.SemaphoreType.DMA((4,)),
        ],
        compiler_params=pltpu.CompilerParams(
            collective_id=0, has_side_effects=True, vmem_limit_bytes=61 << 20
        ),
        cost_estimate=pl.CostEstimate(
            flops=2 * pairs * (window + unknowns), bytes_accessed=8 << 20, transcendentals=0
        ),
    )(
        currents, excitation, couplings.reshape(slots * unknowns, unknowns), block_inverses,
        neighbours, charge_map, potential, lag_profile,
    )
    residual = excitation.astype(f32) - fields
    updated = (currents.astype(f32) + correction).astype(bf16)
    return (updated, residual)


def solution(mesh):
    in_specs = (
        P("clus", "tm", None),
        P("clus", "tm", None),
        P("clus", None),
        P(),
        P(),
        P("clus", None, None),
        P(),
        P(),
    )
    out_specs = (P("clus", "tm", None), P("clus", "tm", None))
    return jax.shard_map(
        on_device, mesh=mesh, in_specs=in_specs, out_specs=out_specs, check_vma=False
    )
```

```python
import functools

import jax
import jax.numpy as jnp
from jax import lax
from jax.experimental import pallas as pl
from jax.experimental.pallas import tpu as pltpu
from jax.sharding import PartitionSpec as P

GROUP = 16
CHARGE_GROUP = 4
PIECES = 8
MESH = pl.DeviceIdType.MESH


def sweep_kernel(
    n_tm, n_clus, own_hbm, exc_hbm, coup_hbm, binv_hbm, neighbours, cmap, pot, profile,
    upd, res,
    ext, filt, toep, lower, coup, binv, exc, base, before, totals,
    send, sib_sem, edge_sem, prev_sem, sib_prev_sem, edge_prev_sem, total_send, total_recv,
    load_sem,
):
    i, c = lax.axis_index("tm"), lax.axis_index("clus")
    per_dev, steps, unknowns = own_hbm.shape
    slots, _, window = toep.shape
    lags = profile.shape[1]
    patches = cmap.shape[1]
    groups = per_dev // GROUP
    size = CHARGE_GROUP * steps
    core = lax.rem(c, 2)
    sibling = c + 1 - 2 * core
    beyond = lax.rem(c + 2 * core - 1 + n_clus, n_clus)
    wraps = (c == 0) | (c == n_clus - 1)
    has_prev, has_later = i > 0, i < n_tm - 1
    later = lax.rem(i + 1, n_tm)
    piece = per_dev // PIECES
    even = lax.rem(i, 2) == 0

    def wrap_over_tm(j):
        return wraps & has_later & (even | (j < 5 * PIECES // 8))

    def prev_over_clus(j):
        return has_prev & (jnp.logical_not(wraps) | (even & (j >= 5 * PIECES // 8)))

    from_beyond, from_sibling = 2 * core, 2 - 2 * core

    barrier = pltpu.get_barrier_semaphore()
    for other in (sibling, beyond):
        pl.semaphore_signal(barrier, inc=1, device_id=(i, other), device_id_type=MESH)
    for by in range(1, n_tm):
        pl.semaphore_signal(
            barrier, inc=1, device_id=(lax.rem(i + by, n_tm), c), device_id_type=MESH
        )
    pl.semaphore_wait(barrier, n_tm + 1)

    def remote(src, dst, sent, received, tm, clus):
        return pltpu.make_async_remote_copy(
            src_ref=src, dst_ref=dst, send_sem=sent, recv_sem=received,
            device_id=(tm, clus), device_id_type=MESH,
        )

    def mine(j):
        return own_hbm.at[pl.ds(j * piece, piece)]

    def new(region, j):
        return ext.at[pl.ds(region * per_dev + j * piece, piece), pl.ds(lags, steps)]

    def old(region, j):
        return ext.at[pl.ds(region * per_dev + j * piece, piece), pl.ds(0, lags)]

    def to_edge(j):
        return remote(
            mine(j), new(from_sibling, j), send.at[0, j], edge_sem.at[j], i, beyond
        )

    def to_later(j):
        return remote(mine(j), old(1, j), send.at[1, j], prev_sem.at[j], later, c)

    def prev_to_sib(j):
        return remote(
            old(1, j), old(from_beyond, j), send.at[2, j], sib_prev_sem.at[j], i, sibling
        )

    def prev_to_edge(j):
        return remote(
            old(1, j), old(from_sibling, j), send.at[3, j], edge_prev_sem.at[j], i, beyond
        )

    def edge_to_later(j):
        return remote(
            new(from_beyond, j), old(from_beyond, j), send.at[4, j], edge_prev_sem.at[j],
            later, c,
        )

    to_sib = remote(
        own_hbm, ext.at[pl.ds(from_beyond * per_dev, per_dev), pl.ds(lags, steps)],
        send.at[5, 0], sib_sem.at[0], i, sibling,
    )
    for j in range(PIECES):
        to_edge(j).start()

        @pl.when(has_later)
        def _():
            to_later(j).start()

    to_sib.start()

    own_rows = (pl.ds(per_dev, per_dev), pl.ds(lags, steps))
    load_own = pltpu.make_async_copy(own_hbm, ext.at[own_rows], load_sem.at[0])
    loads = [
        pltpu.make_async_copy(exc_hbm, exc, load_sem.at[1]),
        pltpu.make_async_copy(coup_hbm, coup, load_sem.at[2]),
        pltpu.make_async_copy(binv_hbm, binv, load_sem.at[3]),
    ]
    load_own.start()
    for load in loads:
        load.start()

    ext[3 * per_dev] = jnp.zeros((window, unknowns), ext.dtype)

    @pl.when(jnp.logical_not(has_prev))
    def _():
        ext[pl.ds(0, 3 * per_dev), pl.ds(0, lags)] = jnp.zeros(
            (3 * per_dev, lags, unknowns), ext.dtype
        )

    load_own.wait()
    sums = jnp.sum(ext[own_rows].astype(jnp.float32), axis=1)
    totals[n_tm] = jnp.dot(
        sums, cmap[...].astype(jnp.float32), precision=lax.Precision.HIGHEST,
        preferred_element_type=jnp.float32,
    )

    def total_to(by):
        return remote(
            totals.at[n_tm], totals.at[by], total_send.at[by], total_recv.at[by],
            lax.rem(i + by, n_tm), c,
        )

    for by in range(1, n_tm):

        @pl.when(i + by < n_tm)
        def _():
            total_to(by).start()

    lag = lax.broadcasted_iota(jnp.int32, (lags, window), 0)
    place = lax.broadcasted_iota(jnp.int32, (lags, window), 1)
    turn = jnp.where(lag + place == lags, 1.0, 0.0).astype(jnp.bfloat16)
    turned = jnp.dot(profile[...], turn, preferred_element_type=jnp.float32)
    for k in range(slots):
        line = jnp.broadcast_to(turned[k : k + 1], (steps, window))
        toep[k] = pltpu.roll(line, 0, 1, stride=1, stride_axis=0).astype(toep.dtype)

    row = lax.broadcasted_iota(jnp.int32, (size, size), 0)
    col = lax.broadcasted_iota(jnp.int32, (size, size), 1)
    keep = (row >= col) & (row // steps == col // steps)
    lower[...] = jnp.where(keep, 1.0, 0.0).astype(lower.dtype)

    for j in range(PIECES):

        @pl.when(has_prev)
        def _():
            to_later(j).wait_recv()
            prev_to_sib(j).start()

        to_edge(j).wait_recv()

        @pl.when(prev_over_clus(j))
        def _():
            prev_to_edge(j).start()

        @pl.when(wrap_over_tm(j))
        def _():
            edge_to_later(j).start()

    before[...] = jnp.zeros(before.shape, before.dtype)
    for by in range(1, n_tm):

        @pl.when(i >= by)
        def _():
            total_to(by).wait_recv()
            before[...] += totals[by]

    for load in loads:
        load.wait()

    def charge_group(group, carry):
        first = group * CHARGE_GROUP
        rows = ext[pl.ds(per_dev + first, CHARGE_GROUP), pl.ds(lags, steps)].reshape(size, unknowns)
        incr = jnp.dot(rows, cmap[...], preferred_element_type=jnp.float32)
        high = incr.astype(jnp.bfloat16)
        rest = (incr - high.astype(jnp.float32)).astype(jnp.bfloat16)
        sums = jnp.dot(
            lower[...], jnp.concatenate([high, rest], axis=1), preferred_element_type=jnp.float32
        )
        running = (sums[:, :patches] + sums[:, patches:]).reshape(CHARGE_GROUP, steps, patches)
        charge = (running + before[pl.ds(first, CHARGE_GROUP)][:, None, :]).astype(jnp.bfloat16)
        field = jnp.dot(
            charge.reshape(size, patches), pot[...], preferred_element_type=jnp.float32
        )
        place = pl.ds(first, CHARGE_GROUP)
        field = field.reshape(CHARGE_GROUP, steps, unknowns)
        base[place] = exc[place].astype(jnp.float32) - field
        return carry

    lax.fori_loop(0, per_dev // CHARGE_GROUP, charge_group, 0)

    to_sib.wait_recv()
    for j in range(PIECES):

        @pl.when(has_prev)
        def _():
            prev_to_sib(j).wait_recv()
            prev_to_edge(j).wait_recv()

    first_local = (c - 1) * per_dev
    total = per_dev * n_clus

    def place_of(cluster, slot):
        at = neighbours[cluster, slot]
        if total & (total - 1) == 0:
            to = (at - first_local) & (total - 1)
        else:
            to = lax.rem(at - first_local + total, total)
        return jnp.where(at < 0, 3 * per_dev, jnp.minimum(to, 3 * per_dev))

    def sweep_group(group, carry):
        first = group * GROUP
        for k in range(slots):
            for n in range(0, GROUP, 2):
                one = ext[place_of(first + n, k)]
                two = ext[place_of(first + n + 1, k)]
                both = jnp.concatenate([one, two], axis=1)
                out = jnp.dot(toep[k], both, preferred_element_type=jnp.float32)
                out = out.astype(jnp.bfloat16)
                lanes = pl.ds(k * unknowns, unknowns)
                filt[pl.ds(n * steps, steps), lanes] = out[:, :unknowns]
                filt[pl.ds((n + 1) * steps, steps), lanes] = out[:, unknowns:]
        near = jnp.dot(filt[...], coup[...], preferred_element_type=jnp.float32)
        place = pl.ds(first, GROUP)
        residual = base[place] - near.reshape(GROUP, steps, unknowns)
        res[place] = residual
        rounded = residual.astype(jnp.bfloat16)
        rows = ext[pl.ds(per_dev + first, GROUP), pl.ds(lags, steps)]
        for n in range(GROUP):
            step = jnp.dot(rounded[n], binv[first + n], preferred_element_type=jnp.float32)
            upd[first + n] = (rows[n].astype(jnp.float32) + step).astype(upd.dtype)
        return carry

    lax.fori_loop(0, groups, sweep_group, 0)

    to_sib.wait_send()
    for by in range(1, n_tm):

        @pl.when(i + by < n_tm)
        def _():
            total_to(by).wait_send()

    for j in range(PIECES):
        to_edge(j).wait_send()

        @pl.when(has_later)
        def _():
            to_later(j).wait_send()

        @pl.when(has_prev)
        def _():
            prev_to_sib(j).wait_send()

        @pl.when(prev_over_clus(j))
        def _():
            prev_to_edge(j).wait_send()

        @pl.when(wrap_over_tm(j))
        def _():
            edge_to_later(j).wait_send()


def on_device(
    currents, excitation, neighbours, lag_profile, couplings, block_inverses, charge_map, potential
):
    per_dev, steps, unknowns = currents.shape
    slots, lags = lag_profile.shape
    window = steps + lags
    patches = charge_map.shape[1]
    n_tm, n_clus = lax.axis_size("tm"), lax.axis_size("clus")
    vmem = pl.BlockSpec(memory_space=pltpu.VMEM)
    smem = pl.BlockSpec(memory_space=pltpu.SMEM)
    hbm = pl.BlockSpec(memory_space=pltpu.HBM)
    size = CHARGE_GROUP * steps
    pairs = per_dev * slots * steps * unknowns
    bf16, f32 = jnp.bfloat16, jnp.float32
    return pl.pallas_call(
        functools.partial(sweep_kernel, n_tm, n_clus),
        in_specs=[hbm] * 4 + [smem, vmem, vmem, vmem],
        out_specs=[vmem, vmem],
        out_shape=[
            pltpu.VMEM(currents.shape, bf16),
            pltpu.VMEM(currents.shape, f32),
        ],
        scratch_shapes=[
            pltpu.VMEM((3 * per_dev + 1, window, unknowns), bf16),
            pltpu.VMEM((GROUP * steps, slots * unknowns), bf16),
            pltpu.VMEM((slots, steps, window), bf16),
            pltpu.VMEM((size, size), bf16),
            pltpu.VMEM((slots * unknowns, unknowns), bf16),
            pltpu.VMEM(block_inverses.shape, bf16),
            pltpu.VMEM(excitation.shape, bf16),
            pltpu.VMEM(currents.shape, f32),
            pltpu.VMEM((per_dev, patches), f32),
            pltpu.VMEM((n_tm + 1, per_dev, patches), f32),
            pltpu.SemaphoreType.DMA((6, PIECES)),
            pltpu.SemaphoreType.DMA((1,)),
            pltpu.SemaphoreType.DMA((PIECES,)),
            pltpu.SemaphoreType.DMA((PIECES,)),
            pltpu.SemaphoreType.DMA((PIECES,)),
            pltpu.SemaphoreType.DMA((PIECES,)),
            pltpu.SemaphoreType.DMA((n_tm,)),
            pltpu.SemaphoreType.DMA((n_tm,)),
            pltpu.SemaphoreType.DMA((4,)),
        ],
        compiler_params=pltpu.CompilerParams(
            collective_id=0, has_side_effects=True, vmem_limit_bytes=61 << 20
        ),
        cost_estimate=pl.CostEstimate(
            flops=2 * pairs * (window + unknowns), bytes_accessed=8 << 20, transcendentals=0
        ),
    )(
        currents, excitation, couplings.reshape(slots * unknowns, unknowns), block_inverses,
        neighbours, charge_map, potential, lag_profile,
    )


def solution(mesh):
    in_specs = (
        P("clus", "tm", None),
        P("clus", "tm", None),
        P("clus", None),
        P(),
        P(),
        P("clus", None, None),
        P(),
        P(),
    )
    out_specs = (P("clus", "tm", None), P("clus", "tm", None))
    return jax.shard_map(
        on_device, mesh=mesh, in_specs=in_specs, out_specs=out_specs, check_vma=False
    )
```

```python
import functools

import jax
import jax.numpy as jnp
from jax import lax
from jax.experimental import pallas as pl
from jax.experimental.pallas import tpu as pltpu
from jax.sharding import PartitionSpec as P

GROUP = 16
CHARGE_GROUP = 4
PIECES = 8
MESH = pl.DeviceIdType.MESH


def sweep_kernel(
    n_tm, n_clus, own_hbm, exc_hbm, coup_hbm, binv_hbm, neighbours, cmap, pot, profile,
    upd, res,
    ext, filt, toep, lower, coup, binv, exc, base, before, totals,
    send, sib_sem, edge_sem, prev_sem, sib_prev_sem, edge_prev_sem, total_send, total_recv,
    load_sem,
):
    i, c = lax.axis_index("tm"), lax.axis_index("clus")
    per_dev, steps, unknowns = own_hbm.shape
    slots, _, window = toep.shape
    lags = profile.shape[1]
    patches = cmap.shape[1]
    groups = per_dev // GROUP
    size = CHARGE_GROUP * steps
    core = lax.rem(c, 2)
    sibling = c + 1 - 2 * core
    beyond = lax.rem(c + 2 * core - 1 + n_clus, n_clus)
    wraps = (c == 0) | (c == n_clus - 1)
    has_prev, has_later = i > 0, i < n_tm - 1
    later = lax.rem(i + 1, n_tm)
    piece = per_dev // PIECES
    even = lax.rem(i, 2) == 0

    def wrap_over_tm(j):
        return wraps & has_later & (even | (j < 3 * PIECES // 4))

    def prev_over_clus(j):
        return has_prev & (jnp.logical_not(wraps) | (even & (j >= 3 * PIECES // 4)))

    from_beyond, from_sibling = 2 * core, 2 - 2 * core

    barrier = pltpu.get_barrier_semaphore()
    for other in (sibling, beyond):
        pl.semaphore_signal(barrier, inc=1, device_id=(i, other), device_id_type=MESH)
    for by in range(1, n_tm):
        pl.semaphore_signal(
            barrier, inc=1, device_id=(lax.rem(i + by, n_tm), c), device_id_type=MESH
        )
    pl.semaphore_wait(barrier, n_tm + 1)

    def remote(src, dst, sent, received, tm, clus):
        return pltpu.make_async_remote_copy(
            src_ref=src, dst_ref=dst, send_sem=sent, recv_sem=received,
            device_id=(tm, clus), device_id_type=MESH,
        )

    def mine(j):
        return own_hbm.at[pl.ds(j * piece, piece)]

    def new(region, j):
        return ext.at[pl.ds(region * per_dev + j * piece, piece), pl.ds(lags, steps)]

    def old(region, j):
        return ext.at[pl.ds(region * per_dev + j * piece, piece), pl.ds(0, lags)]

    def to_edge(j):
        return remote(
            mine(j), new(from_sibling, j), send.at[0, j], edge_sem.at[j], i, beyond
        )

    def to_later(j):
        return remote(mine(j), old(1, j), send.at[1, j], prev_sem.at[j], later, c)

    def prev_to_sib(j):
        return remote(
            old(1, j), old(from_beyond, j), send.at[2, j], sib_prev_sem.at[j], i, sibling
        )

    def prev_to_edge(j):
        return remote(
            old(1, j), old(from_sibling, j), send.at[3, j], edge_prev_sem.at[j], i, beyond
        )

    def edge_to_later(j):
        return remote(
            new(from_beyond, j), old(from_beyond, j), send.at[4, j], edge_prev_sem.at[j],
            later, c,
        )

    to_sib = remote(
        own_hbm, ext.at[pl.ds(from_beyond * per_dev, per_dev), pl.ds(lags, steps)],
        send.at[5, 0], sib_sem.at[0], i, sibling,
    )
    for j in range(PIECES):
        to_edge(j).start()

        @pl.when(has_later)
        def _():
            to_later(j).start()

    to_sib.start()

    own_rows = (pl.ds(per_dev, per_dev), pl.ds(lags, steps))
    load_own = pltpu.make_async_copy(own_hbm, ext.at[own_rows], load_sem.at[0])
    loads = [
        pltpu.make_async_copy(exc_hbm, exc, load_sem.at[1]),
        pltpu.make_async_copy(coup_hbm, coup, load_sem.at[2]),
        pltpu.make_async_copy(binv_hbm, binv, load_sem.at[3]),
    ]
    load_own.start()
    for load in loads:
        load.start()

    ext[3 * per_dev] = jnp.zeros((window, unknowns), ext.dtype)

    @pl.when(jnp.logical_not(has_prev))
    def _():
        ext[pl.ds(0, 3 * per_dev), pl.ds(0, lags)] = jnp.zeros(
            (3 * per_dev, lags, unknowns), ext.dtype
        )

    load_own.wait()
    sums = jnp.sum(ext[own_rows].astype(jnp.float32), axis=1)
    totals[n_tm] = jnp.dot(
        sums, cmap[...].astype(jnp.float32), precision=lax.Precision.HIGHEST,
        preferred_element_type=jnp.float32,
    )

    def total_to(by):
        return remote(
            totals.at[n_tm], totals.at[by], total_send.at[by], total_recv.at[by],
            lax.rem(i + by, n_tm), c,
        )

    for by in range(1, n_tm):

        @pl.when(i + by < n_tm)
        def _():
            total_to(by).start()

    lag = lax.broadcasted_iota(jnp.int32, (lags, window), 0)
    place = lax.broadcasted_iota(jnp.int32, (lags, window), 1)
    turn = jnp.where(lag + place == lags, 1.0, 0.0).astype(jnp.bfloat16)
    turned = jnp.dot(profile[...], turn, preferred_element_type=jnp.float32)
    for k in range(slots):
        line = jnp.broadcast_to(turned[k : k + 1], (steps, window))
        toep[k] = pltpu.roll(line, 0, 1, stride=1, stride_axis=0).astype(toep.dtype)

    row = lax.broadcasted_iota(jnp.int32, (size, size), 0)
    col = lax.broadcasted_iota(jnp.int32, (size, size), 1)
    keep = (row >= col) & (row // steps == col // steps)
    lower[...] = jnp.where(keep, 1.0, 0.0).astype(lower.dtype)

    before[...] = jnp.zeros(before.shape, before.dtype)
    for by in range(1, n_tm):

        @pl.when(i >= by)
        def _():
            total_to(by).wait_recv()
            before[...] += totals[by]

    for load in loads:
        load.wait()

    def charge_group(group):
        first = group * CHARGE_GROUP
        rows = ext[pl.ds(per_dev + first, CHARGE_GROUP), pl.ds(lags, steps)].reshape(size, unknowns)
        incr = jnp.dot(rows, cmap[...], preferred_element_type=jnp.float32)
        high = incr.astype(jnp.bfloat16)
        rest = (incr - high.astype(jnp.float32)).astype(jnp.bfloat16)
        sums = jnp.dot(
            lower[...], jnp.concatenate([high, rest], axis=1), preferred_element_type=jnp.float32
        )
        running = (sums[:, :patches] + sums[:, patches:]).reshape(CHARGE_GROUP, steps, patches)
        charge = (running + before[pl.ds(first, CHARGE_GROUP)][:, None, :]).astype(jnp.bfloat16)
        field = jnp.dot(
            charge.reshape(size, patches), pot[...], preferred_element_type=jnp.float32
        )
        place = pl.ds(first, CHARGE_GROUP)
        field = field.reshape(CHARGE_GROUP, steps, unknowns)
        base[place] = exc[place].astype(jnp.float32) - field

    for j in range(PIECES):

        @pl.when(has_prev)
        def _():
            to_later(j).wait_recv()
            prev_to_sib(j).start()

        to_edge(j).wait_recv()

        @pl.when(prev_over_clus(j))
        def _():
            prev_to_edge(j).start()

        @pl.when(wrap_over_tm(j))
        def _():
            edge_to_later(j).start()

        for group in range(j, per_dev // CHARGE_GROUP, PIECES):
            charge_group(group)

    to_sib.wait_recv()
    for j in range(PIECES):

        @pl.when(has_prev)
        def _():
            prev_to_sib(j).wait_recv()
            prev_to_edge(j).wait_recv()

    first_local = (c - 1) * per_dev
    total = per_dev * n_clus

    def place_of(cluster, slot):
        at = neighbours[cluster, slot]
        if total & (total - 1) == 0:
            to = (at - first_local) & (total - 1)
        else:
            to = lax.rem(at - first_local + total, total)
        return jnp.where(at < 0, 3 * per_dev, jnp.minimum(to, 3 * per_dev))

    def sweep_group(group, carry):
        first = group * GROUP
        for k in range(slots):
            for n in range(0, GROUP, 2):
                one = ext[place_of(first + n, k)]
                two = ext[place_of(first + n + 1, k)]
                both = jnp.concatenate([one, two], axis=1)
                out = jnp.dot(toep[k], both, preferred_element_type=jnp.float32)
                out = out.astype(jnp.bfloat16)
                lanes = pl.ds(k * unknowns, unknowns)
                filt[pl.ds(n * steps, steps), lanes] = out[:, :unknowns]
                filt[pl.ds((n + 1) * steps, steps), lanes] = out[:, unknowns:]
        near = jnp.dot(filt[...], coup[...], preferred_element_type=jnp.float32)
        place = pl.ds(first, GROUP)
        residual = base[place] - near.reshape(GROUP, steps, unknowns)
        res[place] = residual
        rounded = residual.astype(jnp.bfloat16)
        rows = ext[pl.ds(per_dev + first, GROUP), pl.ds(lags, steps)]
        for n in range(GROUP):
            step = jnp.dot(rounded[n], binv[first + n], preferred_element_type=jnp.float32)
            upd[first + n] = (rows[n].astype(jnp.float32) + step).astype(upd.dtype)
        return carry

    lax.fori_loop(0, groups, sweep_group, 0)

    to_sib.wait_send()
    for by in range(1, n_tm):

        @pl.when(i + by < n_tm)
        def _():
            total_to(by).wait_send()

    for j in range(PIECES):
        to_edge(j).wait_send()

        @pl.when(has_later)
        def _():
            to_later(j).wait_send()

        @pl.when(has_prev)
        def _():
            prev_to_sib(j).wait_send()

        @pl.when(prev_over_clus(j))
        def _():
            prev_to_edge(j).wait_send()

        @pl.when(wrap_over_tm(j))
        def _():
            edge_to_later(j).wait_send()


def on_device(
    currents, excitation, neighbours, lag_profile, couplings, block_inverses, charge_map, potential
):
    per_dev, steps, unknowns = currents.shape
    slots, lags = lag_profile.shape
    window = steps + lags
    patches = charge_map.shape[1]
    n_tm, n_clus = lax.axis_size("tm"), lax.axis_size("clus")
    vmem = pl.BlockSpec(memory_space=pltpu.VMEM)
    smem = pl.BlockSpec(memory_space=pltpu.SMEM)
    hbm = pl.BlockSpec(memory_space=pltpu.HBM)
    size = CHARGE_GROUP * steps
    pairs = per_dev * slots * steps * unknowns
    bf16, f32 = jnp.bfloat16, jnp.float32
    return pl.pallas_call(
        functools.partial(sweep_kernel, n_tm, n_clus),
        in_specs=[hbm] * 4 + [smem, vmem, vmem, vmem],
        out_specs=[vmem, vmem],
        out_shape=[
            pltpu.VMEM(currents.shape, bf16),
            pltpu.VMEM(currents.shape, f32),
        ],
        scratch_shapes=[
            pltpu.VMEM((3 * per_dev + 1, window, unknowns), bf16),
            pltpu.VMEM((GROUP * steps, slots * unknowns), bf16),
            pltpu.VMEM((slots, steps, window), bf16),
            pltpu.VMEM((size, size), bf16),
            pltpu.VMEM((slots * unknowns, unknowns), bf16),
            pltpu.VMEM(block_inverses.shape, bf16),
            pltpu.VMEM(excitation.shape, bf16),
            pltpu.VMEM(currents.shape, f32),
            pltpu.VMEM((per_dev, patches), f32),
            pltpu.VMEM((n_tm + 1, per_dev, patches), f32),
            pltpu.SemaphoreType.DMA((6, PIECES)),
            pltpu.SemaphoreType.DMA((1,)),
            pltpu.SemaphoreType.DMA((PIECES,)),
            pltpu.SemaphoreType.DMA((PIECES,)),
            pltpu.SemaphoreType.DMA((PIECES,)),
            pltpu.SemaphoreType.DMA((PIECES,)),
            pltpu.SemaphoreType.DMA((n_tm,)),
            pltpu.SemaphoreType.DMA((n_tm,)),
            pltpu.SemaphoreType.DMA((4,)),
        ],
        compiler_params=pltpu.CompilerParams(
            collective_id=0, has_side_effects=True, vmem_limit_bytes=61 << 20
        ),
        cost_estimate=pl.CostEstimate(
            flops=2 * pairs * (window + unknowns), bytes_accessed=8 << 20, transcendentals=0
        ),
    )(
        currents, excitation, couplings.reshape(slots * unknowns, unknowns), block_inverses,
        neighbours, charge_map, potential, lag_profile,
    )


def solution(mesh):
    in_specs = (
        P("clus", "tm", None),
        P("clus", "tm", None),
        P("clus", None),
        P(),
        P(),
        P("clus", None, None),
        P(),
        P(),
    )
    out_specs = (P("clus", "tm", None), P("clus", "tm", None))
    return jax.shard_map(
        on_device, mesh=mesh, in_specs=in_specs, out_specs=out_specs, check_vma=False
    )
```
